256 devices in a mesh: dp: 8 (over x, y_lo), mp: 32 (over y_hi, z, core).
Axes of the slice: x: 4, y: 4 (y_hi: 2, y_lo: 2; y = y_hi * 2 + y_lo), z: 8, core: 2. Of those that a mesh axis runs over, the one named last changes fastest.
Arguments:
- tokens: bfloat16 [2048, 4096], P('dp', 'mp'), may hold values from -6 to 6
- cotangent: bfloat16 [2048, 4096], P('dp', 'mp'), may hold values from -6 to 6
- gate_weight: bfloat16 [4096, 16384], P('dp', 'mp'), may hold values from -0.1875 to 0.1875
- up_weight: bfloat16 [4096, 16384], P('dp', 'mp'), may hold values from -0.1875 to 0.1875
- down_weight: bfloat16 [16384, 4096], P('mp', 'dp'), may hold values from -0.09375 to 0.09375
- gate_mask: int32 [32, 128], P('dp', 'mp'), may hold values from 0 to 1, as said below
- up_mask: int32 [32, 128], P('dp', 'mp'), may hold values from 0 to 1, as said below
- down_mask: int32 [128, 32], P('mp', 'dp'), may hold values from 0 to 1, as said below
Outputs:
- layer_out: bfloat16 [2048, 4096], P('dp', 'mp')
- token_grad: bfloat16 [2048, 4096], P('dp', 'mp')
- gate_grad: bfloat16 [4096, 16384], P('dp', 'mp')
- up_grad: bfloat16 [4096, 16384], P('dp', 'mp')
- down_grad: bfloat16 [16384, 4096], P('mp', 'dp')
The draws below stay inside these ranges and needn't reach their ends.
Inputs may be any that keep to these rules, and one draw needn't show every extreme that they name: `gate_mask`: each device's part of the mask (4 x 4 blocks) has 1 to 8 nonzero blocks; in every draw all parts of one index of mp, chosen by the seed, have exactly 8, the same index for the three masks. `up_mask`: each device's part of the mask (4 x 4 blocks) has 1 to 8 nonzero blocks; in every draw all parts of one index of mp, chosen by the seed, have exactly 8, the same index for the three masks. `down_mask`: each device's part of the mask (4 x 4 blocks) has 1 to 8 nonzero blocks; in every draw all parts of one index of mp, chosen by the seed, have exactly 8, the same index for the three masks.
All inputs are finite; a program needn't handle non-finite values.
Results may differ from the reference program's by a relative error of at most 0.017.
Values may be sent and summed in bfloat16 or wider, within the bound.
A program may use at most 128 MiB of HBM per device.

```python
import math
import jax
import jax.numpy as jnp
from jax import lax

D = 4096
F = 16384
BLK = 128
TOK_DEV = 256
TOKENS = 2048
ROW_TILES = 4
COL_TILES = 4
CAP = 8


def live_tiles(key, salt_value):
    dp_shards = D // BLK // ROW_TILES
    mp_shards = F // BLK // COL_TILES
    tile_total = ROW_TILES * COL_TILES
    own_key = jax.random.fold_in(key, salt_value)
    counts = jax.random.randint(jax.random.fold_in(own_key, 1), (dp_shards, mp_shards), 1, CAP)
    full_column = jax.random.randint(jax.random.fold_in(key, 101), (), 0, mp_shards)
    counts = jnp.where(jnp.arange(mp_shards)[None, :] == full_column, CAP, counts)
    scores = jax.random.randint(jax.random.fold_in(own_key, 2), (dp_shards, mp_shards, tile_total), 0, 1048576)
    scores = scores * tile_total + jnp.arange(tile_total, dtype=jnp.int32)[None, None, :]
    ranking = jnp.argsort(jnp.argsort(scores, axis=-1), axis=-1)
    return (ranking < counts[:, :, None]).astype(jnp.int32)


def upper_layout(key, salt_value):
    dp_shards = D // BLK // ROW_TILES
    mp_shards = F // BLK // COL_TILES
    grid = live_tiles(key, salt_value).reshape(dp_shards, mp_shards, ROW_TILES, COL_TILES)
    return grid.transpose(0, 2, 1, 3).reshape(D // BLK, F // BLK)


def draw_gate_mask(key, part):
    return upper_layout(key, 1)


def draw_up_mask(key, part):
    return upper_layout(key, 2)


def draw_down_mask(key, part):
    dp_shards = D // BLK // ROW_TILES
    mp_shards = F // BLK // COL_TILES
    grid = live_tiles(key, 3).reshape(dp_shards, mp_shards, COL_TILES, ROW_TILES)
    return grid.transpose(1, 2, 0, 3).reshape(F // BLK, D // BLK)


def steps_of(rng, dims, pieces, low, largest):
    factor_of, own = 1.0, jax.random.fold_in(rng, 6)
    for axis_at, blocks in pieces:
        heights = jnp.exp(jax.random.uniform(jax.random.fold_in(own, axis_at), (blocks,), jnp.float32, low / len(pieces), largest / len(pieces)))
        factor_of = factor_of * jnp.repeat(heights, dims[axis_at] // blocks).reshape([-1 if axis == axis_at else 1 for axis in range(len(dims))])
    return factor_of


def noise(key, extent, spread, most, split=(), kind=jnp.bfloat16):
    array = spread * jax.random.normal(key, extent, jnp.float32)
    if split:
        array = array * steps_of(key, extent, split, -0.22, 0.18)
    return jnp.clip(array, -most, most).astype(kind)


def setup_inputs(seed: int = 0) -> dict:
    streams_of = jax.random.split(jax.random.key(seed), 9)
    tokens = noise(streams_of[0], (TOKENS, D), 1.0, 6.0, ((0, 8), (1, 32)))
    cotangent = noise(streams_of[1], (TOKENS, D), 1.0, 6.0, ((0, 8), (1, 32)))
    gate_weight = noise(streams_of[2], (D, F), (D // 4) ** -0.5, 0.1875, ((0, 8), (1, 32)))
    up_weight = noise(streams_of[3], (D, F), (D // 4) ** -0.5, 0.1875, ((0, 8), (1, 32)))
    down_weight = noise(streams_of[4], (F, D), (F // 4) ** -0.5, 0.09375, ((0, 32), (1, 8)))
    gate_mask = draw_gate_mask(jax.random.fold_in(streams_of[8], 71), 0)
    up_mask = draw_up_mask(jax.random.fold_in(streams_of[8], 71), 0)
    down_mask = draw_down_mask(jax.random.fold_in(streams_of[8], 71), 0)
    return dict(tokens=tokens, cotangent=cotangent, gate_weight=gate_weight, up_weight=up_weight, down_weight=down_weight, gate_mask=gate_mask, up_mask=up_mask, down_mask=down_mask)


def expand(mask_table):
    return jnp.repeat(jnp.repeat(mask_table, BLK, axis=0), BLK, axis=1).astype(jnp.bfloat16)

def rounded(values):
    lowered = values.astype(jnp.bfloat16)
    lowered = lax.optimization_barrier(lowered)
    return lowered.astype(jnp.float32)

def reference(tokens, cotangent, gate_weight, up_weight, down_weight, gate_mask, up_mask, down_mask):
    gate_eff = gate_weight * expand(gate_mask)
    up_eff = up_weight * expand(up_mask)
    down_eff = down_weight * expand(down_mask)
    gate_pre = jnp.dot(tokens, gate_eff, preferred_element_type=jnp.float32)
    up_pre = jnp.dot(tokens, up_eff, preferred_element_type=jnp.float32)
    sigmoid_gate = 1.0 / (1.0 + jnp.exp(-gate_pre))
    activated = gate_pre * sigmoid_gate
    hidden = (activated * up_pre).astype(jnp.bfloat16)
    layer_out = jnp.dot(hidden, down_eff, preferred_element_type=jnp.float32).astype(jnp.bfloat16)
    hidden_grad = jnp.dot(cotangent, down_eff.T, preferred_element_type=jnp.float32)
    gate_delta = (hidden_grad * up_pre * sigmoid_gate * (1.0 + gate_pre * (1.0 - sigmoid_gate))).astype(jnp.bfloat16)
    up_delta = (hidden_grad * activated).astype(jnp.bfloat16)
    token_grad = (jnp.dot(gate_delta, gate_eff.T, preferred_element_type=jnp.float32) + jnp.dot(up_delta, up_eff.T, preferred_element_type=jnp.float32)).astype(jnp.bfloat16)

    def group_terms(totals, group_index):
        first_row = (group_index * TOK_DEV).astype(jnp.int32)
        rows_in = lax.dynamic_slice_in_dim(tokens, first_row, TOK_DEV, 0)
        rows_cot = lax.dynamic_slice_in_dim(cotangent, first_row, TOK_DEV, 0)
        rows_gate = lax.dynamic_slice_in_dim(gate_delta, first_row, TOK_DEV, 0)
        rows_up = lax.dynamic_slice_in_dim(up_delta, first_row, TOK_DEV, 0)
        rows_hidden = lax.dynamic_slice_in_dim(hidden, first_row, TOK_DEV, 0)
        part_gate = rounded(jnp.dot(rows_in.T, rows_gate, preferred_element_type=jnp.float32))
        part_up = rounded(jnp.dot(rows_in.T, rows_up, preferred_element_type=jnp.float32))
        part_down = rounded(jnp.dot(rows_hidden.T, rows_cot, preferred_element_type=jnp.float32))
        return ((totals[0] + part_gate, totals[1] + part_up, totals[2] + part_down), None)
    initial = (jnp.zeros((D, F), jnp.float32), jnp.zeros((D, F), jnp.float32), jnp.zeros((F, D), jnp.float32))
    group_count = TOKENS // TOK_DEV
    totals, _ = lax.scan(group_terms, initial, jnp.arange(group_count, dtype=jnp.int32))
    grad_scale = 1.0 / math.sqrt(TOKENS)
    gate_grad = (totals[0] * grad_scale * expand(gate_mask).astype(jnp.float32)).astype(jnp.bfloat16)
    up_grad = (totals[1] * grad_scale * expand(up_mask).astype(jnp.float32)).astype(jnp.bfloat16)
    down_grad = (totals[2] * grad_scale * expand(down_mask).astype(jnp.float32)).astype(jnp.bfloat16)
    return (layer_out, token_grad, gate_grad, up_grad, down_grad)
```

```python
import math

import jax
import jax.numpy as jnp
from jax import lax
from jax.experimental import pallas as pl
from jax.experimental.pallas import tpu as pltpu
from jax.sharding import PartitionSpec as P

BLK = 128
F32 = jnp.float32
BF16 = jnp.bfloat16
NX, NZ = 4, 8
SLOTS = 8
TILES = 16
SCALE = 1.0 / math.sqrt(2048)


def kernel(
    tok, cot, gate_w, up_w, down_w, gate_m, up_m, down_m,
    layer_out, token_grad, gate_g, up_g, down_g,
    feats, packed_0, packed_1, packed_2, meta, meta_sm, w_up, w_down, pre, act, psend, precv, hid, deltas,
    tiles, gpack, gtransit, gfinal, gown, outs, ocore, oring, oyh, oyl,
    yl_s, yl_r, yh_s, yh_r, z_s, z_r, c_s, c_r,
    ws_s, wf_s, w_r, meta_s, meta_r, meta_l, p_s, p_r,
    gt_s, gt_r, gf_s, gf_r, oc_s, oc_r, oz_s, oz_r, oyh_s, oyh_r, oyl_s, oyl_r,
):
    dp, mp = lax.axis_index("dp"), lax.axis_index("mp")
    x, yl = dp // 2, dp % 2
    yh, z, c = mp // 16, (mp % 16) // 2, mp % 2

    def dev(dx=0, dz=0, flip_yl=False, flip_yh=False, flip_c=False):
        yl_, yh_, c_ = (1 - yl if flip_yl else yl), (1 - yh if flip_yh else yh), (1 - c if flip_c else c)
        return (((x + dx) % NX) * 2 + yl_, yh_ * 16 + ((z + dz) % NZ) * 2 + c_)

    other_yl, other_yh, other_c = dev(flip_yl=True), dev(flip_yh=True), dev(flip_c=True)
    x_right, x_left, x_far = dev(dx=1), dev(dx=NX - 1), dev(dx=2)
    z_next = (dev(dz=1), dev(dz=NZ - 1))

    def remote(src, dst, send, recv, to):
        return pltpu.make_async_remote_copy(
            src_ref=src, dst_ref=dst, send_sem=send, recv_sem=recv,
            device_id=to, device_id_type=pl.DeviceIdType.MESH,
        )

    def arrived(dst, send, recv):
        remote(dst, dst, send, recv, other_c).wait_recv()

    def loop(n, body):
        def step(i, carry):
            body(i)
            return carry

        lax.fori_loop(0, n, step, 0)

    barrier = pltpu.get_barrier_semaphore()
    partners = (other_yl, other_yh, other_c, x_right, x_left, x_far, *z_next)
    for to in partners:
        pl.semaphore_signal(barrier, inc=1, device_id=to, device_id_type=pl.DeviceIdType.MESH)
    pl.semaphore_wait(barrier, len(partners))

    holder = (z // 2) % 2 == yl

    def holds(at):
        return (at // 2) % 2 == yl

    def chunk(at_yh, at_z, at_c):
        return at_yh * 8 + (at_z // 4) * 4 + (at_z % 2) * 2 + at_c

    home = chunk(yh, z, c)

    def send_z(tc, at_z, w, e, hop):
        q, h = chunk((yh + w) % 2, at_z, c), (yl + e) % 2
        for d in range(2):
            remote(feats.at[tc, q, h], feats.at[tc, q, h], z_s.at[d, hop - 1, tc, w, e], z_r.at[d, hop - 1, tc, w, e], z_next[d]).start()

    def send_core(tc, at_z, w, e):
        q, h = chunk((yh + w) % 2, at_z, c), (yl + e) % 2
        remote(feats.at[tc, q, h], feats.at[tc, q, h], c_s.at[tc, q // 2, e], c_r.at[tc, q // 2, e], other_c).start()

    def yh_piece(tc, e):
        q, h = home, (yl + e) % 2
        return remote(feats.at[tc, q, h], feats.at[tc, q, h], yh_s.at[tc, e], yh_r.at[tc, e], other_yh)

    def tokens_own(tc, ref):
        @pl.when(holder)
        def _():
            feats[tc, home, yl] = ref[...]
            yh_piece(tc, 0).start()
            send_z(tc, z, 0, 0, 1)
            send_core(tc, z, 0, 0)

        @pl.when(jnp.logical_not(holder))
        def _():
            remote(ref, feats.at[tc, home, yl], yl_s.at[tc], yl_r.at[tc], other_yl).start()

    def tokens_second(tc):
        @pl.when(holder)
        def _():
            arrived(feats.at[tc, home, 1 - yl], yl_s.at[tc], yl_r.at[tc])
            yh_piece(tc, 1).start()
            send_z(tc, z, 0, 1, 1)
            send_core(tc, z, 0, 1)

    def tokens_third(tc):
        @pl.when(holder)
        def _():
            for e in range(2):
                arrived(feats.at[tc, chunk(1 - yh, z, c), (yl + e) % 2], yh_s.at[tc, e], yh_r.at[tc, e])
                send_z(tc, z, 1, e, 1)
                send_core(tc, z, 1, e)

    def last_hop(d, w):
        return jnp.where(w == d, 4, 3)

    def tokens_hop(tc, hop):
        def step(i):
            w, e = i // 2, i % 2
            for d in range(2):
                at_z = (z + (NZ - hop if d == 0 else hop)) % NZ

                @pl.when(jnp.logical_and(holds(at_z), hop <= last_hop(d, w)))
                def _():
                    q, h = chunk((yh + w) % 2, at_z, c), (yl + e) % 2
                    piece = feats.at[tc, q, h]
                    arrived(piece, z_s.at[d, hop - 1, tc, w, e], z_r.at[d, hop - 1, tc, w, e])

                    @pl.when(hop < last_hop(d, w))
                    def _():
                        remote(piece, piece, z_s.at[d, hop, tc, w, e], z_r.at[d, hop, tc, w, e], z_next[d]).start()

                    send_core(tc, at_z, w, e)

        loop(4, step)

    def tokens_from_core(tc):
        def step(i):
            j, e = i // 2, i % 2
            arrived(feats.at[tc, j * 2 + 1 - c, (yl + e) % 2], c_s.at[tc, j, e], c_r.at[tc, j, e])

        loop(16, step)

    packed = (packed_0, packed_1, packed_2)
    masks, weights = (gate_m, up_m, down_m), (gate_w, up_w, down_w)
    lane = lax.broadcasted_iota(jnp.int32, (8, BLK), 0) * BLK + lax.broadcasted_iota(jnp.int32, (8, BLK), 1)

    def pack(m, table):
        for t in range(TILES):
            r, k = t // 4, t % 4
            tiles[t] = weights[m][r * BLK:(r + 1) * BLK, k * BLK:(k + 1) * BLK]
        count = jnp.int32(0)
        ids = [jnp.int32(0)] * SLOTS
        for t in range(TILES):
            kept = masks[m][t // 4, t % 4] > 0
            for s in range(min(t + 1, SLOTS)):
                ids[s] = jnp.where(jnp.logical_and(kept, count == s), t, ids[s])
            table = jnp.where(lane == m * BLK + t, jnp.where(kept, count, SLOTS), table)
            count = count + jnp.where(kept, 1, 0)
        for s in range(SLOTS):
            table = jnp.where(lane == m * BLK + TILES + s, ids[s], table)
            packed[m][x, s] = tiles[ids[s]]
        for at, to in ((0, x_right), (1, x_left)):
            for h in range(2):
                half = packed[m].at[x, pl.ds(h * 4, 4)]
                remote(half, half, ws_s.at[at, m, h], w_r.at[at, m, h], to).start()
        return table

    def forward_weights(m):
        for at, h, origin, to in ((0, 0, NX - 1, x_right), (1, 1, 1, x_left)):
            half = packed[m].at[(x + origin) % NX, pl.ds(h * 4, 4)]
            arrived(half, ws_s.at[at, m, h], w_r.at[at, m, h])
            remote(half, half, wf_s.at[m, h], w_r.at[2, m, h], to).start()

    def unpack(m):
        for at, origin in ((0, NX - 1), (1, 1), (2, 2)):
            for h in range(2):
                if at == 2 or at != h:
                    arrived(packed[m].at[(x + origin) % NX, pl.ds(h * 4, 4)], ws_s.at[0, m, h], w_r.at[at, m, h])

        def tile(i):
            xx, r = i // 4, i % 4
            for t in range(4):
                value = packed[m][xx, meta_sm[xx, m, r * 4 + t]]
                if m < 2:
                    row = pl.multiple_of(xx * 512 + r * BLK, BLK)
                    w_up[m, pl.ds(row, BLK), t * BLK:(t + 1) * BLK] = value
                else:
                    w_down[xx, pl.ds(pl.multiple_of(r * BLK, BLK), BLK), t * BLK:(t + 1) * BLK] = value

        loop(16, tile)

    tokens_own(0, tok)
    for xx in range(NX):
        for m in range(3):
            packed[m][xx, SLOTS] = jnp.zeros((BLK, BLK), BF16)
    table = pack(0, jnp.zeros((8, BLK), jnp.int32))
    tokens_own(1, cot)
    tokens_second(0)
    table = pack(1, table)
    table = pack(2, table)
    meta[x] = table
    for at, to in ((0, x_right), (1, x_left), (2, x_far)):
        remote(meta.at[x], meta.at[x], meta_s.at[at], meta_r.at[at], to).start()
    tokens_third(0)
    tokens_hop(0, 1)
    tokens_second(1)
    tokens_hop(0, 2)
    forward_weights(0)
    tokens_third(1)
    tokens_hop(0, 3)
    forward_weights(1)
    for at, origin in ((0, NX - 1), (1, 1), (2, 2)):
        arrived(meta.at[(x + origin) % NX], meta_s.at[at], meta_r.at[at])
    tables = pltpu.make_async_copy(meta, meta_sm, meta_l)
    tables.start()
    tokens_hop(0, 4)
    tables.wait()
    tokens_hop(1, 1)

    def features(tc, h):
        return jnp.concatenate([feats[tc, q, h] for q in range(16)], axis=1)

    def exchange(m):
        def rows(h):
            if m < 2:
                total = jnp.dot(features(0, h), w_up[m], preferred_element_type=F32)
            else:
                total = jnp.zeros((256, 512), F32)
                for xx in range(NX):
                    left = jnp.concatenate([feats[1, xx * 4 + k, h] for k in range(4)], axis=1)
                    total += lax.dot_general(left, w_down[xx], (((1,), (1,)), ((), ())), preferred_element_type=F32)
            pre[m, h] = total
            psend[m, h] = total.astype(BF16)
            remote(psend.at[m, h], precv.at[m, h], p_s.at[m, h], p_r.at[m, h], other_yl).start()

        loop(2, rows)

    def exchanged(m):
        for h in range(2):
            arrived(precv.at[m, h], p_s.at[m, h], p_r.at[m, h])

    tokens_from_core(0)
    unpack(0)
    exchange(0)
    forward_weights(2)
    tokens_hop(1, 2)
    unpack(1)
    exchange(1)
    tokens_hop(1, 3)
    tokens_hop(1, 4)
    tokens_from_core(1)
    unpack(2)
    exchange(2)

    exchanged(0)
    exchanged(1)

    def activate(i):
        h, rows = i // 4, pl.ds(pl.multiple_of((i % 4) * 64, 64), 64)
        g = pre[0, h, rows, :] + precv[0, h, rows, :].astype(F32)
        u = pre[1, h, rows, :] + precv[1, h, rows, :].astype(F32)
        sigmoid = 1.0 / (1.0 + jnp.exp(-g))
        activated = g * sigmoid
        hid[h, rows, :] = (activated * u).astype(BF16)
        act[0, h, rows, :] = u * sigmoid * (1.0 + g * (1.0 - sigmoid))
        act[1, h, rows, :] = activated

    loop(8, activate)

    contract_rows = (((0,), (0,)), ((), ()))

    def grad_partial(m, rel):
        xx = (x + rel) % NX
        side = jnp.concatenate([feats[0 if m < 2 else 1, xx * 4 + k].reshape(512, BLK) for k in range(4)], axis=1)

        def col(k):
            if m < 2:
                right = deltas[m].reshape(512, 512)
                grad = lax.dot_general(side, right, contract_rows, preferred_element_type=F32)
            else:
                grad = lax.dot_general(hid[...].reshape(512, 512), side, contract_rows, preferred_element_type=F32)
            return grad

        grad = col(0).astype(BF16)
        for r in range(4):
            for t in range(4):
                tiles[r * 4 + t] = grad[r * BLK:(r + 1) * BLK, t * BLK:(t + 1) * BLK]
        for s in range(SLOTS):
            gpack[rel, m, s] = tiles[meta_sm[xx, m, TILES + s]]

    lows, highs = pl.ds(0, 4), pl.ds(4, 4)

    def grad_send(m):
        def part(i):
            rel = (i + 2) % NX
            grad_partial(m, rel)

            @pl.when(rel == 2)
            def _():
                remote(gpack.at[2, m, lows], gtransit.at[0, m], gt_s.at[0, m], gt_r.at[0, m], x_right).start()
                remote(gpack.at[2, m, highs], gtransit.at[1, m], gt_s.at[1, m], gt_r.at[1, m], x_left).start()

            @pl.when(rel == 1)
            def _():
                remote(gpack.at[1, m, highs], gfinal.at[0, m, highs], gf_s.at[0, m, 1], gf_r.at[0, m, 1], x_right).start()

            @pl.when(rel == 3)
            def _():
                remote(gpack.at[3, m, lows], gfinal.at[1, m, lows], gf_s.at[1, m, 0], gf_r.at[1, m, 0], x_left).start()

        loop(NX, part)

    def grad_transit(m):
        for at, rel, h, to in ((0, 1, 0, x_right), (1, 3, 1, x_left)):
            part = pl.ds(h * 4, 4)
            arrived(gtransit.at[at, m], gt_s.at[at, m], gt_r.at[at, m])
            gpack[rel, m, part] = (gpack[rel, m, part].astype(F32) + gtransit[at, m].astype(F32)).astype(BF16)
            remote(gpack.at[rel, m, part], gfinal.at[at, m, part], gf_s.at[at, m, h], gf_r.at[at, m, h], to).start()

    def grad_finish(m, out):
        for at in range(2):
            for h in range(2):
                arrived(gfinal.at[at, m, pl.ds(h * 4, 4)], gf_s.at[at, m, h], gf_r.at[at, m, h])
        for s in range(SLOTS):
            total = gpack[0, m, s].astype(F32) + gfinal[0, m, s].astype(F32) + gfinal[1, m, s].astype(F32)
            gown[m, s] = (total * SCALE).astype(BF16)
        gown[m, SLOTS] = jnp.zeros((BLK, BLK), BF16)
        for t in range(TILES):
            r, k = t // 4, t % 4
            out[r * BLK:(r + 1) * BLK, k * BLK:(k + 1) * BLK] = gown[m, meta_sm[x, m, t]]

    def out_partial(o):
        def part(i):
            xx, h = i // 2, i % 2
            if o == 0:
                term = jnp.dot(hid[h], w_down[xx], preferred_element_type=F32)
            else:
                rows = pl.ds(pl.multiple_of(xx * 512, 512), 512)
                along = (((1,), (1,)), ((), ()))
                term = lax.dot_general(deltas[0, h], w_up[0, rows, :], along, preferred_element_type=F32)
                term += lax.dot_general(deltas[1, h], w_up[1, rows, :], along, preferred_element_type=F32)
            term = term.astype(BF16)
            for k in range(4):
                outs[o, xx * 4 + k, h] = term[:, k * BLK:(k + 1) * BLK]

        loop(8, part)

        def send(j):
            remote(outs.at[o, j * 2 + 1 - c], ocore.at[o, j], oc_s.at[o, j], oc_r.at[o, j], other_c).start()

        loop(8, send)

    def out_core(o):
        def step(j):
            arrived(ocore.at[o, j], oc_s.at[o, j], oc_r.at[o, j])
            q = j * 2 + c
            outs[o, q] = (outs[o, q].astype(F32) + ocore[o, j].astype(F32)).astype(BF16)

        loop(8, step)

    def out_hop(o, hop):
        def step(i):
            w, h = i // 2, i % 2
            for d in range(2):
                at_z = (z + (hop if d == 0 else NZ - hop)) % NZ

                @pl.when(jnp.logical_and(holds(at_z), hop <= last_hop(d, w)))
                def _():
                    q = chunk((yh + w) % 2, at_z, c)
                    j = q // 2

                    @pl.when(hop < last_hop(d, w))
                    def _():
                        arrived(oring.at[d, o, j, h], oz_s.at[o, j, h], oz_r.at[d, o, j, h])
                        outs[o, q, h] = (outs[o, q, h].astype(F32) + oring[d, o, j, h].astype(F32)).astype(BF16)

                    remote(outs.at[o, q, h], oring.at[d, o, j, h], oz_s.at[o, j, h], oz_r.at[d, o, j, h], z_next[d]).start()

        loop(4, step)

    def out_home(o):
        @pl.when(holder)
        def _():
            for w in (1, 0):
                for h in range(2):
                    q = chunk((yh + w) % 2, z, c)
                    j = q // 2
                    for d in range(2):
                        arrived(oring.at[d, o, j, h], oz_s.at[o, j, h], oz_r.at[d, o, j, h])
                    total = outs[o, q, h].astype(F32) + oring[0, o, j, h].astype(F32) + oring[1, o, j, h].astype(F32)
                    outs[o, q, h] = total.astype(BF16)
                    if w == 1:
                        remote(outs.at[o, q, h], oyh.at[o, h], oyh_s.at[o, h], oyh_r.at[o, h], other_yh).start()

    def out_last(o, out):
        @pl.when(holder)
        def _():
            for e in (1, 0):
                h = (yl + e) % 2
                arrived(oyh.at[o, h], oyh_s.at[o, h], oyh_r.at[o, h])
                total = (outs[o, home, h].astype(F32) + oyh[o, h].astype(F32)).astype(BF16)
                if e == 1:
                    outs[o, home, h] = total
                    remote(outs.at[o, home, h], oyl.at[o], oyl_s.at[o], oyl_r.at[o], other_yl).start()
                else:
                    out[...] = total

    def out_other(o, out):
        @pl.when(jnp.logical_not(holder))
        def _():
            arrived(oyl.at[o], oyl_s.at[o], oyl_r.at[o])
            out[...] = oyl[o]

    grad_send(2)
    out_partial(0)
    grad_transit(2)
    out_core(0)
    out_hop(0, 4)
    out_hop(0, 3)
    exchanged(2)

    def delta(i):
        h, rows = i // 4, pl.ds(pl.multiple_of((i % 4) * 64, 64), 64)
        hg = pre[2, h, rows, :] + precv[2, h, rows, :].astype(F32)
        deltas[0, h, rows, :] = (hg * act[0, h, rows, :]).astype(BF16)
        deltas[1, h, rows, :] = (hg * act[1, h, rows, :]).astype(BF16)

    loop(8, delta)
    grad_send(0)
    out_hop(0, 2)
    grad_send(1)
    out_hop(0, 1)
    grad_transit(0)
    out_partial(1)
    grad_transit(1)
    out_core(1)
    out_hop(1, 4)
    out_home(0)
    out_hop(1, 3)
    grad_finish(2, down_g)
    out_hop(1, 2)
    out_last(0, layer_out)
    out_hop(1, 1)
    out_home(1)
    grad_finish(0, gate_g)
    grad_finish(1, up_g)
    out_last(1, token_grad)
    out_other(0, layer_out)
    out_other(1, token_grad)

    def left(src, send):
        remote(src, src, send, z_r.at[0, 0, 0, 0, 0], other_c).wait_send()

    piece = feats.at[0, 0, 0]
    for tc in range(2):

        @pl.when(holder)
        def _():
            for e in range(2):
                left(piece, yh_s.at[tc, e])

                for w in range(2):
                    for d in range(2):
                        left(piece, z_s.at[d, 0, tc, w, e])

        @pl.when(jnp.logical_not(holder))
        def _():
            left(piece, yl_s.at[tc])

        def hops(i):
            w, e = i // 2, i % 2
            for hop in range(1, 4):
                for d in range(2):
                    at_z = (z + (NZ - hop if d == 0 else hop)) % NZ

                    @pl.when(jnp.logical_and(holds(at_z), hop < last_hop(d, w)))
                    def _():
                        left(piece, z_s.at[d, hop, tc, w, e])

        loop(4, hops)

        def cores(i):
            left(piece, c_s.at[tc, i // 2, i % 2])

        loop(16, cores)
        o = tc

        def ocores(j):
            left(ocore.at[0, 0], oc_s.at[o, j])

            @pl.when(jnp.logical_not(jnp.logical_and(holder, jnp.logical_and((j // 2) % 2 == z // 4, j % 2 == z % 2))))
            def _():
                for h in range(2):
                    left(piece, oz_s.at[o, j, h])

        loop(8, ocores)

        @pl.when(holder)
        def _():
            for h in range(2):
                left(piece, oyh_s.at[o, h])
            left(piece, oyl_s.at[o])

    half = gtransit.at[0, 0]
    for at in range(3):
        left(meta.at[0], meta_s.at[at])
    for m in range(3):
        for h in range(2):
            for at in range(2):
                left(half, ws_s.at[at, m, h])
                left(half, gf_s.at[at, m, h])
            left(half, wf_s.at[m, h])
            left(half, gt_s.at[h, m])
            left(psend.at[0, 0], p_s.at[m, h])


def body(tokens, cotangent, gate_weight, up_weight, down_weight, gate_mask, up_mask, down_mask):
    vmem, smem = pl.BlockSpec(memory_space=pltpu.VMEM), pl.BlockSpec(memory_space=pltpu.SMEM)
    dma = pltpu.SemaphoreType.DMA
    shapes = (tokens, cotangent, gate_weight, up_weight, down_weight)
    return pl.pallas_call(
        kernel,
        out_shape=tuple(jax.ShapeDtypeStruct(a.shape, a.dtype) for a in shapes),
        in_specs=[vmem] * 5 + [smem] * 3,
        out_specs=(vmem,) * 5,
        scratch_shapes=[
            pltpu.VMEM((2, 16, 2, 256, BLK), BF16),
            *[pltpu.VMEM((NX, SLOTS + 1, BLK, BLK), BF16)] * 3,
            pltpu.VMEM((NX, 8, BLK), jnp.int32),
            pltpu.SMEM((NX, 8, BLK), jnp.int32),
            pltpu.VMEM((2, 2048, 512), BF16),
            pltpu.VMEM((NX, 512, 512), BF16),
            pltpu.VMEM((3, 2, 256, 512), F32),
            pltpu.VMEM((2, 2, 256, 512), F32),
            pltpu.VMEM((3, 2, 256, 512), BF16),
            pltpu.VMEM((3, 2, 256, 512), BF16),
            pltpu.VMEM((2, 256, 512), BF16),
            pltpu.VMEM((2, 2, 256, 512), BF16),
            pltpu.VMEM((TILES, BLK, BLK), BF16),
            pltpu.VMEM((NX, 3, SLOTS, BLK, BLK), BF16),
            pltpu.VMEM((2, 3, 4, BLK, BLK), BF16),
            pltpu.VMEM((2, 3, SLOTS, BLK, BLK), BF16),
            pltpu.VMEM((3, SLOTS + 1, BLK, BLK), BF16),
            pltpu.VMEM((2, 16, 2, 256, BLK), BF16),
            pltpu.VMEM((2, 8, 2, 256, BLK), BF16),
            pltpu.VMEM((2, 2, 8, 2, 256, BLK), BF16),
            pltpu.VMEM((2, 2, 256, BLK), BF16),
            pltpu.VMEM((2, 256, BLK), BF16),
            dma((2,)), dma((2,)), dma((2, 2)), dma((2, 2)),
            dma((2, 4, 2, 2, 2)), dma((2, 4, 2, 2, 2)),
            dma((2, 8, 2)), dma((2, 8, 2)),
            dma((2, 3, 2)), dma((3, 2)), dma((3, 3, 2)),
            dma((3,)), dma((3,)), dma(()),
            dma((3, 2)), dma((3, 2)),
            dma((2, 3)), dma((2, 3)), dma((2, 3, 2)), dma((2, 3, 2)),
            dma((2, 8)), dma((2, 8)),
            dma((2, 8, 2)), dma((2, 2, 8, 2)),
            dma((2, 2)), dma((2, 2)), dma((2,)), dma((2,)),
        ],
        compiler_params=pltpu.CompilerParams(
            collective_id=0, has_side_effects=True, vmem_limit_bytes=58 * 2**20
        ),
        cost_estimate=pl.CostEstimate(flops=9_663_676_416, bytes_accessed=4 * 2**20, transcendentals=262144),
    )(tokens, cotangent, gate_weight, up_weight, down_weight, gate_mask, up_mask, down_mask)


def solution(mesh):
    up, down = P("dp", "mp"), P("mp", "dp")
    return jax.shard_map(
        body,
        mesh=mesh,
        in_specs=(up, up, up, up, down, up, up, down),
        out_specs=(up, up, up, up, down),
        check_vma=False,
    )
```

```python
import math

import jax
import jax.numpy as jnp
from jax import lax
from jax.experimental import pallas as pl
from jax.experimental.pallas import tpu as pltpu
from jax.sharding import PartitionSpec as P

BLK = 128
F32 = jnp.float32
BF16 = jnp.bfloat16
NX, NZ = 4, 8
SLOTS = 8
TILES = 16
SCALE = 1.0 / math.sqrt(2048)


def kernel(
    tok, cot, gate_w, up_w, down_w, gate_m, up_m, down_m,
    layer_out, token_grad, gate_g, up_g, down_g,
    feats, packed_0, packed_1, packed_2, meta, meta_sm, w_up, w_down, pre, act, psend, precv, hid, deltas,
    tiles, gpack, gtransit, gfinal, gown, outs, ocore, oring, ohome, oyh, oyl,
    yl_s, yl_r, yh_s, yh_r, z_s, z_r, c_s, c_r,
    ws_s, wf_s, w_r, meta_s, meta_r, meta_l, p_s, p_r,
    gt_s, gt_r, gf_s, gf_r, oc_s, oc_r, oz_s, oz_r, oh_s, oh_r, oyh_s, oyh_r, oyl_s, oyl_r,
):
    dp, mp = lax.axis_index("dp"), lax.axis_index("mp")
    x, yl = dp // 2, dp % 2
    yh, z, c = mp // 16, (mp % 16) // 2, mp % 2

    def dev(dx=0, dz=0, flip_yl=False, flip_yh=False, flip_c=False):
        yl_, yh_, c_ = (1 - yl if flip_yl else yl), (1 - yh if flip_yh else yh), (1 - c if flip_c else c)
        return (((x + dx) % NX) * 2 + yl_, yh_ * 16 + ((z + dz) % NZ) * 2 + c_)

    other_yl, other_yh, other_c = dev(flip_yl=True), dev(flip_yh=True), dev(flip_c=True)
    x_right, x_left, x_far = dev(dx=1), dev(dx=NX - 1), dev(dx=2)
    z_up, z_down = dev(dz=1), dev(dz=NZ - 1)
    z_to = dev(dz=jnp.where(c == 0, 1, NZ - 1))

    def remote(src, dst, send, recv, to):
        return pltpu.make_async_remote_copy(
            src_ref=src, dst_ref=dst, send_sem=send, recv_sem=recv,
            device_id=to, device_id_type=pl.DeviceIdType.MESH,
        )

    def arrived(dst, send, recv):
        remote(dst, dst, send, recv, other_c).wait_recv()

    def loop(n, body):
        def step(i, carry):
            body(i)
            return carry

        lax.fori_loop(0, n, step, 0)

    barrier = pltpu.get_barrier_semaphore()
    partners = (other_yl, other_yh, other_c, x_right, x_left, x_far, z_up, z_down)
    for to in partners:
        pl.semaphore_signal(barrier, inc=1, device_id=to, device_id_type=pl.DeviceIdType.MESH)
    pl.semaphore_wait(barrier, len(partners))

    holder = (z // 2) % 2 == yl

    def holds(at):
        return (at // 2) % 2 == yl

    def chunk(at_yh, at_z, at_c):
        return at_yh * 8 + (at_z // 4) * 4 + (at_z % 2) * 2 + at_c

    home = chunk(yh, z, c)

    def behind(hops):
        return (z + jnp.where(c == 0, NZ - hops, hops)) % NZ

    def ahead(hops):
        return (z + jnp.where(c == 0, hops, NZ - hops)) % NZ

    def last_hop(w):
        return jnp.where(w == c, 4, 3)

    def by_core(up, w):
        return jnp.where(up <= jnp.where(w == 0, 4, 3), 0, 1)

    def send_core(tc, q, e):
        piece = feats.at[tc, q, (yl + e) % 2]
        remote(piece, piece, c_s.at[tc, q, e], c_r.at[tc, q, e], other_c).start()

    def send_yh(tc, e):
        piece = feats.at[tc, home, (yl + e) % 2]
        remote(piece, piece, yh_s.at[tc, e], yh_r.at[tc, e], other_yh).start()

    def tokens_own(tc, ref):
        @pl.when(holder)
        def _():
            feats[tc, home, yl] = ref[...]
            send_yh(tc, 0)

        @pl.when(jnp.logical_not(holder))
        def _():
            remote(ref, feats.at[tc, home, yl], yl_s.at[tc], yl_r.at[tc], other_yl).start()

    def token_waves(first, end):
        def wave(t, carry):
            def send_z(piece, tc, w, e, o, hop):
                remote(piece, piece, z_s.at[hop, tc, w, e, o], z_r.at[hop, tc, w, e, o], z_to).start()

            @pl.when(jnp.logical_and(holder, t < 16))
            def _():
                tc, w, e, o = t // 8, (t // 4) % 2, (t // 2) % 2, t % 2
                q = chunk((yh + w) % 2, z, (c + o) % 2)
                piece = feats.at[tc, q, (yl + e) % 2]

                @pl.when(o == 1)
                def _():
                    arrived(piece, c_s.at[tc, q, e], c_r.at[tc, q, e])

                @pl.when(o == 0)
                def _():
                    @pl.when(jnp.logical_and(w == 0, e == 1))
                    def _():
                        arrived(piece, yl_s.at[tc], yl_r.at[tc])
                        send_yh(tc, 1)

                    @pl.when(w == 1)
                    def _():
                        arrived(piece, yh_s.at[tc, e], yh_r.at[tc, e])

                    send_core(tc, q, e)

                send_z(piece, tc, w, e, o, 0)

            for hop in (4, 3, 2, 1):
                p, at_z = t - 2 * hop, behind(hop)
                tc, w, e, o = p // 8, (p // 4) % 2, (p // 2) % 2, p % 2
                takes = jnp.logical_and(holds(at_z), hop <= last_hop(w))

                @pl.when(jnp.logical_and(takes, jnp.logical_and(p >= 0, p < 16)))
                def _():
                    q = chunk((yh + w) % 2, at_z, (c + o) % 2)
                    piece = feats.at[tc, q, (yl + e) % 2]
                    arrived(piece, z_s.at[hop - 1, tc, w, e, o], z_r.at[hop - 1, tc, w, e, o])
                    if hop < 4:

                        @pl.when(hop < last_hop(w))
                        def _():
                            send_z(piece, tc, w, e, o, hop)

                    send_core(tc, q, e)

            return carry

        lax.fori_loop(first, end, wave, 0)

    def via_core(j):
        up = (z - ((j // 2) % 2 * 4 + yl * 2 + j % 2) + NZ) % NZ
        return jnp.logical_and(up != 0, by_core(up, (j // 4 + yh) % 2) != c)

    def tokens_from_core(tc):
        def step(i):
            q, e = i // 2, i % 2

            @pl.when(via_core(q // 2))
            def _():
                arrived(feats.at[tc, q, (yl + e) % 2], c_s.at[tc, q, e], c_r.at[tc, q, e])

        loop(32, step)

    packed = (packed_0, packed_1, packed_2)
    masks, weights = (gate_m, up_m, down_m), (gate_w, up_w, down_w)
    lane = lax.broadcasted_iota(jnp.int32, (8, BLK), 0) * BLK + lax.broadcasted_iota(jnp.int32, (8, BLK), 1)

    def pack(m, table):
        for t in range(TILES):
            r, k = t // 4, t % 4
            tiles[t] = weights[m][r * BLK:(r + 1) * BLK, k * BLK:(k + 1) * BLK]
        count = jnp.int32(0)
        ids = [jnp.int32(0)] * SLOTS
        for t in range(TILES):
            kept = masks[m][t // 4, t % 4] > 0
            for s in range(min(t + 1, SLOTS)):
                ids[s] = jnp.where(jnp.logical_and(kept, count == s), t, ids[s])
            table = jnp.where(lane == m * BLK + t, jnp.where(kept, count, SLOTS), table)
            count = count + jnp.where(kept, 1, 0)
        for s in range(SLOTS):
            table = jnp.where(lane == m * BLK + TILES + s, ids[s], table)
            packed[m][x, s] = tiles[ids[s]]
        for at, to in ((0, x_right), (1, x_left)):
            for h in range(2):
                half = packed[m].at[x, pl.ds(h * 4, 4)]
                remote(half, half, ws_s.at[at, m, h], w_r.at[at, m, h], to).start()
        return table

    def forward_weights(m):
        for at, h, origin, to in ((0, 0, NX - 1, x_right), (1, 1, 1, x_left)):
            half = packed[m].at[(x + origin) % NX, pl.ds(h * 4, 4)]
            arrived(half, ws_s.at[at, m, h], w_r.at[at, m, h])
            remote(half, half, wf_s.at[m, h], w_r.at[2, m, h], to).start()

    def unpack(m):
        for at, origin in ((0, NX - 1), (1, 1), (2, 2)):
            for h in range(2):
                if at == 2 or at != h:
                    arrived(packed[m].at[(x + origin) % NX, pl.ds(h * 4, 4)], ws_s.at[0, m, h], w_r.at[at, m, h])

        def tile(i):
            xx, r = i // 4, i % 4
            for t in range(4):
                value = packed[m][xx, meta_sm[xx, m, r * 4 + t]]
                if m < 2:
                    row = pl.multiple_of(xx * 512 + r * BLK, BLK)
                    w_up[m, pl.ds(row, BLK), t * BLK:(t + 1) * BLK] = value
                else:
                    w_down[xx, pl.ds(pl.multiple_of(r * BLK, BLK), BLK), t * BLK:(t + 1) * BLK] = value

        loop(16, tile)

    tokens_own(0, tok)
    tokens_own(1, cot)
    token_waves(0, 1)
    table = pack(0, jnp.zeros((8, BLK), jnp.int32))
    token_waves(1, 2)
    table = pack(1, table)
    token_waves(2, 4)
    table = pack(2, table)
    meta[x] = table
    for at, to in ((0, x_right), (1, x_left), (2, x_far)):
        remote(meta.at[x], meta.at[x], meta_s.at[at], meta_r.at[at], to).start()
    token_waves(4, 6)
    for xx in range(NX):
        for m in range(3):
            packed[m][xx, SLOTS] = jnp.zeros((BLK, BLK), BF16)
    token_waves(6, 8)
    forward_weights(0)
    token_waves(8, 10)
    for at, origin in ((0, NX - 1), (1, 1), (2, 2)):
        arrived(meta.at[(x + origin) % NX], meta_s.at[at], meta_r.at[at])
    tables = pltpu.make_async_copy(meta, meta_sm, meta_l)
    tables.start()
    token_waves(10, 13)
    tables.wait()
    unpack(0)
    token_waves(13, 15)
    forward_weights(1)
    token_waves(15, 16)

    def features(tc, h):
        return jnp.concatenate([feats[tc, q, h] for q in range(16)], axis=1)

    def exchange(m):
        def rows(h):
            if m < 2:
                total = jnp.dot(features(0, h), w_up[m], preferred_element_type=F32)
            else:
                total = jnp.zeros((256, 512), F32)
                for xx in range(NX):
                    left = jnp.concatenate([feats[1, xx * 4 + k, h] for k in range(4)], axis=1)
                    total += lax.dot_general(left, w_down[xx], (((1,), (1,)), ((), ())), preferred_element_type=F32)
            pre[m, h] = total
            psend[m, h] = total.astype(BF16)
            remote(psend.at[m, h], precv.at[m, h], p_s.at[m, h], p_r.at[m, h], other_yl).start()

        loop(2, rows)

    def exchanged(m):
        for h in range(2):
            arrived(precv.at[m, h], p_s.at[m, h], p_r.at[m, h])

    tokens_from_core(0)
    exchange(0)
    token_waves(16, 18)
    unpack(1)
    exchange(1)
    token_waves(18, 20)
    forward_weights(2)
    token_waves(20, 24)
    tokens_from_core(1)
    unpack(2)
    exchange(2)

    exchanged(0)
    exchanged(1)

    def activate(i):
        h, rows = i // 4, pl.ds(pl.multiple_of((i % 4) * 64, 64), 64)
        g = pre[0, h, rows, :] + precv[0, h, rows, :].astype(F32)
        u = pre[1, h, rows, :] + precv[1, h, rows, :].astype(F32)
        sigmoid = 1.0 / (1.0 + jnp.exp(-g))
        activated = g * sigmoid
        hid[h, rows, :] = (activated * u).astype(BF16)
        act[0, h, rows, :] = u * sigmoid * (1.0 + g * (1.0 - sigmoid))
        act[1, h, rows, :] = activated

    loop(8, activate)

    contract_rows = (((0,), (0,)), ((), ()))

    def grad_partial(m, rel):
        xx = (x + rel) % NX
        side = jnp.concatenate([feats[0 if m < 2 else 1, xx * 4 + k].reshape(512, BLK) for k in range(4)], axis=1)

        def col(k):
            if m < 2:
                right = deltas[m].reshape(512, 512)
                grad = lax.dot_general(side, right, contract_rows, preferred_element_type=F32)
            else:
                grad = lax.dot_general(hid[...].reshape(512, 512), side, contract_rows, preferred_element_type=F32)
            return grad

        grad = col(0).astype(BF16)
        for r in range(4):
            for t in range(4):
                tiles[r * 4 + t] = grad[r * BLK:(r + 1) * BLK, t * BLK:(t + 1) * BLK]
        for s in range(SLOTS):
            gpack[rel, m, s] = tiles[meta_sm[xx, m, TILES + s]]

    lows, highs = pl.ds(0, 4), pl.ds(4, 4)

    def grad_send(m):
        def part(i):
            rel = (i + 2) % NX
            grad_partial(m, rel)

            @pl.when(rel == 2)
            def _():
                remote(gpack.at[2, m, lows], gtransit.at[0, m], gt_s.at[0, m], gt_r.at[0, m], x_right).start()
                remote(gpack.at[2, m, highs], gtransit.at[1, m], gt_s.at[1, m], gt_r.at[1, m], x_left).start()

            @pl.when(rel == 1)
            def _():
                remote(gpack.at[1, m, highs], gfinal.at[0, m, highs], gf_s.at[0, m, 1], gf_r.at[0, m, 1], x_right).start()

            @pl.when(rel == 3)
            def _():
                remote(gpack.at[3, m, lows], gfinal.at[1, m, lows], gf_s.at[1, m, 0], gf_r.at[1, m, 0], x_left).start()

        loop(NX, part)

    def grad_transit(m):
        for at, rel, h, to in ((0, 1, 0, x_right), (1, 3, 1, x_left)):
            part = pl.ds(h * 4, 4)
            arrived(gtransit.at[at, m], gt_s.at[at, m], gt_r.at[at, m])
            gpack[rel, m, part] = (gpack[rel, m, part].astype(F32) + gtransit[at, m].astype(F32)).astype(BF16)
            remote(gpack.at[rel, m, part], gfinal.at[at, m, part], gf_s.at[at, m, h], gf_r.at[at, m, h], to).start()

    def grad_finish(m, out):
        for at in range(2):
            for h in range(2):
                arrived(gfinal.at[at, m, pl.ds(h * 4, 4)], gf_s.at[at, m, h], gf_r.at[at, m, h])
        for s in range(SLOTS):
            total = gpack[0, m, s].astype(F32) + gfinal[0, m, s].astype(F32) + gfinal[1, m, s].astype(F32)
            gown[m, s] = (total * SCALE).astype(BF16)
        gown[m, SLOTS] = jnp.zeros((BLK, BLK), BF16)
        for t in range(TILES):
            r, k = t // 4, t % 4
            out[r * BLK:(r + 1) * BLK, k * BLK:(k + 1) * BLK] = gown[m, meta_sm[x, m, t]]

    def out_partial(o):
        def part(i):
            xx, h = i // 2, i % 2
            if o == 0:
                term = jnp.dot(hid[h], w_down[xx], preferred_element_type=F32)
            else:
                rows = pl.ds(pl.multiple_of(xx * 512, 512), 512)
                along = (((1,), (1,)), ((), ()))
                term = lax.dot_general(deltas[0, h], w_up[0, rows, :], along, preferred_element_type=F32)
                term += lax.dot_general(deltas[1, h], w_up[1, rows, :], along, preferred_element_type=F32)
            term = term.astype(BF16)
            for k in range(4):
                outs[o, xx * 4 + k, h] = term[:, k * BLK:(k + 1) * BLK]

        loop(8, part)

        def send(j):
            @pl.when(out_via_core(j))
            def _():
                pair = pl.ds(j * 2, 2)
                remote(outs.at[o, pair], ocore.at[o, j], oc_s.at[o, j], oc_r.at[o, j], other_c).start()

        loop(8, send)

    def out_via_core(j):
        up = ((j // 2) % 2 * 4 + yl * 2 + j % 2 - z + NZ) % NZ
        return jnp.logical_and(up != 0, by_core(up, (j // 4 + yh) % 2) != c)

    def out_waves(o, first, end):
        def wave(t, carry):
            for hop in (4, 1, 2, 3):
                p, at_z = t - 2 * (4 - hop), ahead(hop)
                w, cc, h = 1 - p // 4, (p // 2) % 2, p % 2
                takes = jnp.logical_and(holds(at_z), hop <= last_hop(w))

                @pl.when(jnp.logical_and(takes, jnp.logical_and(p >= 0, p < 8)))
                def _():
                    j = chunk((yh + w) % 2, at_z, 0) // 2
                    q = j * 2 + cc

                    @pl.when(p % 4 == 0)
                    def _():
                        arrived(ocore.at[o, j], oc_s.at[o, j], oc_r.at[o, j])

                    total = outs[o, q, h].astype(F32) + ocore[o, j, cc, h].astype(F32)
                    outs[o, q, h] = total.astype(BF16)
                    if hop < 4:

                        @pl.when(hop < last_hop(w))
                        def _():
                            arrived(oring.at[o, j, cc, h], oz_s.at[o, j, cc, h], oz_r.at[o, j, cc, h])
                            outs[o, q, h] = (total + oring[o, j, cc, h].astype(F32)).astype(BF16)

                    remote(outs.at[o, q, h], oring.at[o, j, cc, h], oz_s.at[o, j, cc, h], oz_r.at[o, j, cc, h], z_to).start()

            return carry

        lax.fori_loop(first, end, wave, 0)

    def out_home(o):
        @pl.when(holder)
        def _():
            for w in (1, 0):
                j = chunk((yh + w) % 2, z, 0) // 2
                for own in (0, 1):
                    cc = (c + 1 - own) % 2
                    for h in range(2):
                        q = j * 2 + cc
                        arrived(oring.at[o, j, cc, h], oz_s.at[o, j, cc, h], oz_r.at[o, j, cc, h])
                        outs[o, q, h] = (outs[o, q, h].astype(F32) + oring[o, j, cc, h].astype(F32)).astype(BF16)
                        if own == 0:
                            remote(outs.at[o, q, h], ohome.at[o, w, h], oh_s.at[o, w, h], oh_r.at[o, w, h], other_c).start()
            for w in (1, 0):
                q = chunk((yh + w) % 2, z, c)
                for h in range(2):
                    arrived(ohome.at[o, w, h], oh_s.at[o, w, h], oh_r.at[o, w, h])
                    outs[o, q, h] = (outs[o, q, h].astype(F32) + ohome[o, w, h].astype(F32)).astype(BF16)
                    if w == 1:
                        remote(outs.at[o, q, h], oyh.at[o, h], oyh_s.at[o, h], oyh_r.at[o, h], other_yh).start()

    def out_last(o, out):
        @pl.when(holder)
        def _():
            for e in (1, 0):
                h = (yl + e) % 2
                arrived(oyh.at[o, h], oyh_s.at[o, h], oyh_r.at[o, h])
                total = (outs[o, home, h].astype(F32) + oyh[o, h].astype(F32)).astype(BF16)
                if e == 1:
                    outs[o, home, h] = total
                    remote(outs.at[o, home, h], oyl.at[o], oyl_s.at[o], oyl_r.at[o], other_yl).start()
                else:
                    out[...] = total

    def out_other(o, out):
        @pl.when(jnp.logical_not(holder))
        def _():
            arrived(oyl.at[o], oyl_s.at[o], oyl_r.at[o])
            out[...] = oyl[o]

    out_partial(0)
    grad_send(2)
    out_waves(0, 0, 6)
    grad_transit(2)
    out_waves(0, 6, 14)
    exchanged(2)

    def delta(i):
        h, rows = i // 4, pl.ds(pl.multiple_of((i % 4) * 64, 64), 64)
        hg = pre[2, h, rows, :] + precv[2, h, rows, :].astype(F32)
        deltas[0, h, rows, :] = (hg * act[0, h, rows, :]).astype(BF16)
        deltas[1, h, rows, :] = (hg * act[1, h, rows, :]).astype(BF16)

    loop(8, delta)
    grad_send(0)
    out_partial(1)
    out_waves(1, 0, 2)
    grad_send(1)
    out_waves(1, 2, 6)
    grad_transit(0)
    out_waves(1, 6, 10)
    grad_transit(1)
    out_waves(1, 10, 14)
    out_home(0)
    out_home(1)
    out_last(0, layer_out)
    out_last(1, token_grad)
    grad_finish(2, down_g)
    grad_finish(0, gate_g)
    grad_finish(1, up_g)
    out_other(0, layer_out)
    out_other(1, token_grad)

    def left(src, send):
        remote(src, src, send, z_r.at[0, 0, 0, 0, 0], other_c).wait_send()

    piece = feats.at[0, 0, 0]

    def tokens_left(i):
        tc, w, e, o = i // 8, (i // 4) % 2, (i // 2) % 2, i % 2
        for hop in range(4):
            at_z = behind(hop)

            @pl.when(jnp.logical_and(holds(at_z), hop < last_hop(w)))
            def _():
                left(piece, z_s.at[hop, tc, w, e, o])

    loop(16, tokens_left)

    def to_core_left(i):
        tc, q, e = i // 32, (i // 2) % 16, i % 2
        own = jnp.logical_and((q // 4) % 2 * 4 + yl * 2 + (q // 2) % 2 == z, q % 2 != c)

        @pl.when(jnp.logical_not(jnp.logical_or(via_core(q // 2), own)))
        def _():
            left(piece, c_s.at[tc, q, e])

    loop(64, to_core_left)

    def outs_left(i):
        o, j = i // 8, i % 8
        at_home = (j // 2) % 2 * 4 + yl * 2 + j % 2 == z
        other = out_via_core(j)

        @pl.when(other)
        def _():
            left(ocore.at[0, 0], oc_s.at[o, j])

        @pl.when(jnp.logical_not(jnp.logical_or(other, at_home)))
        def _():
            for cc in range(2):
                for h in range(2):
                    left(piece, oz_s.at[o, j, cc, h])

    loop(16, outs_left)
    for tc in range(2):

        @pl.when(holder)
        def _():
            for e in range(2):
                left(piece, yh_s.at[tc, e])
                left(piece, oyh_s.at[tc, e])
                for w in range(2):
                    left(piece, oh_s.at[tc, w, e])
            left(piece, oyl_s.at[tc])

        @pl.when(jnp.logical_not(holder))
        def _():
            left(piece, yl_s.at[tc])

    half = gtransit.at[0, 0]
    for at in range(3):
        left(meta.at[0], meta_s.at[at])
    for m in range(3):
        for h in range(2):
            for at in range(2):
                left(half, ws_s.at[at, m, h])
                left(half, gf_s.at[at, m, h])
            left(half, wf_s.at[m, h])
            left(half, gt_s.at[h, m])
            left(psend.at[0, 0], p_s.at[m, h])


def body(tokens, cotangent, gate_weight, up_weight, down_weight, gate_mask, up_mask, down_mask):
    vmem, smem = pl.BlockSpec(memory_space=pltpu.VMEM), pl.BlockSpec(memory_space=pltpu.SMEM)
    dma = pltpu.SemaphoreType.DMA
    shapes = (tokens, cotangent, gate_weight, up_weight, down_weight)
    return pl.pallas_call(
        kernel,
        out_shape=tuple(jax.ShapeDtypeStruct(a.shape, a.dtype) for a in shapes),
        in_specs=[vmem] * 5 + [smem] * 3,
        out_specs=(vmem,) * 5,
        scratch_shapes=[
            pltpu.VMEM((2, 16, 2, 256, BLK), BF16),
            *[pltpu.VMEM((NX, SLOTS + 1, BLK, BLK), BF16)] * 3,
            pltpu.VMEM((NX, 8, BLK), jnp.int32),
            pltpu.SMEM((NX, 8, BLK), jnp.int32),
            pltpu.VMEM((2, 2048, 512), BF16),
            pltpu.VMEM((NX, 512, 512), BF16),
            pltpu.VMEM((3, 2, 256, 512), F32),
            pltpu.VMEM((2, 2, 256, 512), F32),
            pltpu.VMEM((3, 2, 256, 512), BF16),
            pltpu.VMEM((3, 2, 256, 512), BF16),
            pltpu.VMEM((2, 256, 512), BF16),
            pltpu.VMEM((2, 2, 256, 512), BF16),
            pltpu.VMEM((TILES, BLK, BLK), BF16),
            pltpu.VMEM((NX, 3, SLOTS, BLK, BLK), BF16),
            pltpu.VMEM((2, 3, 4, BLK, BLK), BF16),
            pltpu.VMEM((2, 3, SLOTS, BLK, BLK), BF16),
            pltpu.VMEM((3, SLOTS + 1, BLK, BLK), BF16),
            pltpu.VMEM((2, 16, 2, 256, BLK), BF16),
            pltpu.VMEM((2, 8, 2, 2, 256, BLK), BF16),
            pltpu.VMEM((2, 8, 2, 2, 256, BLK), BF16),
            pltpu.VMEM((2, 2, 2, 256, BLK), BF16),
            pltpu.VMEM((2, 2, 256, BLK), BF16),
            pltpu.VMEM((2, 256, BLK), BF16),
            dma((2,)), dma((2,)), dma((2, 2)), dma((2, 2)),
            dma((4, 2, 2, 2, 2)), dma((4, 2, 2, 2, 2)),
            dma((2, 16, 2)), dma((2, 16, 2)),
            dma((2, 3, 2)), dma((3, 2)), dma((3, 3, 2)),
            dma((3,)), dma((3,)), dma(()),
            dma((3, 2)), dma((3, 2)),
            dma((2, 3)), dma((2, 3)), dma((2, 3, 2)), dma((2, 3, 2)),
            dma((2, 8)), dma((2, 8)),
            dma((2, 8, 2, 2)), dma((2, 8, 2, 2)),
            dma((2, 2, 2)), dma((2, 2, 2)),
            dma((2, 2)), dma((2, 2)), dma((2,)), dma((2,)),
        ],
        compiler_params=pltpu.CompilerParams(
            collective_id=0, has_side_effects=True, vmem_limit_bytes=58 * 2**20
        ),
        cost_estimate=pl.CostEstimate(flops=9_663_676_416, bytes_accessed=4 * 2**20, transcendentals=262144),
    )(tokens, cotangent, gate_weight, up_weight, down_weight, gate_mask, up_mask, down_mask)


def solution(mesh):
    up, down = P("dp", "mp"), P("mp", "dp")
    return jax.shard_map(
        body,
        mesh=mesh,
        in_specs=(up, up, up, up, down, up, up, down),
        out_specs=(up, up, up, up, down),
        check_vma=False,
    )
```

```python
import math

import jax
import jax.numpy as jnp
from jax import lax
from jax.experimental import pallas as pl
from jax.experimental.pallas import tpu as pltpu
from jax.sharding import PartitionSpec as P

BLK = 128
F32 = jnp.float32
BF16 = jnp.bfloat16
NX, NZ = 4, 8
SLOTS = 8
TILES = 16
SCALE = 1.0 / math.sqrt(2048)


def kernel(
    tok, cot, gate_w, up_w, down_w, gate_m, up_m, down_m,
    layer_out, token_grad, gate_g, up_g, down_g,
    feats, packed_0, packed_1, packed_2, meta, meta_sm, w_up, w_down, pre, act, psend, precv, hid, deltas,
    tiles, gpack, gtransit, gfinal, gown, outs, ocore, oz_0, oz_1, oyh_0, oyh_1, oyl,
    yl_s, yl_r, yh_s, yh_r, z_s, z_r, c_s, c_r,
    ws_s, wf_s, w_r, meta_s, meta_r, meta_l, p_s, p_r,
    gt_s, gt_r, gf_s, gf_r, oc_s, oc_r, oz_s, oz_r, oyh_s, oyh_r, oyl_s, oyl_r,
):
    dp, mp = lax.axis_index("dp"), lax.axis_index("mp")
    x, yl = dp // 2, dp % 2
    yh, z, c = mp // 16, (mp % 16) // 2, mp % 2

    def dev(dx=0, dz=0, flip_yl=False, flip_yh=False, flip_c=False):
        yl_, yh_, c_ = (1 - yl if flip_yl else yl), (1 - yh if flip_yh else yh), (1 - c if flip_c else c)
        return (((x + dx) % NX) * 2 + yl_, yh_ * 16 + ((z + dz) % NZ) * 2 + c_)

    other_yl, other_yh, other_c = dev(flip_yl=True), dev(flip_yh=True), dev(flip_c=True)
    x_right, x_left, x_far = dev(dx=1), dev(dx=NX - 1), dev(dx=2)
    along_z = [dev(dz=k) for k in (1, 7, 2, 6, 3, 5, 4)]

    def remote(src, dst, send, recv, to):
        return pltpu.make_async_remote_copy(
            src_ref=src, dst_ref=dst, send_sem=send, recv_sem=recv,
            device_id=to, device_id_type=pl.DeviceIdType.MESH,
        )

    def arrived(dst, send, recv):
        remote(dst, dst, send, recv, other_c).wait_recv()

    def loop(n, body):
        def step(i, carry):
            body(i)
            return carry

        lax.fori_loop(0, n, step, 0)

    barrier = pltpu.get_barrier_semaphore()
    partners = (other_yl, other_yh, other_c, x_right, x_left, x_far, *along_z)
    for to in partners:
        pl.semaphore_signal(barrier, inc=1, device_id=to, device_id_type=pl.DeviceIdType.MESH)
    pl.semaphore_wait(barrier, len(partners))

    holder = (z // 2) % 2 == yl

    def holds(at):
        return (at // 2) % 2 == yl

    def chunk(at_yh, at_z, at_c):
        return at_yh * 8 + (at_z // 4) * 4 + (at_z % 2) * 2 + at_c

    home = chunk(yh, z, c)

    def homes(i):
        return (z + jnp.where(i % 2 == 1, (i + 1) // 2, NZ - i // 2)) % NZ

    def feature(tc, w, at_z, e):
        return feats.at[tc, chunk((yh + w) % 2, at_z, c), (yl + e) % 2]

    def send_core(tc, w, at_z, e):
        piece, j = feature(tc, w, at_z, e), chunk((yh + w) % 2, at_z, c) // 2
        remote(piece, piece, c_s.at[tc, j, e], c_r.at[tc, j, e], other_c).start()

    def place(at_z):
        return (at_z // 4) * 2 + at_z % 2

    def send_yh(tc, at_z, e):
        piece = feature(tc, 0, at_z, e)
        remote(piece, piece, yh_s.at[tc, place(at_z), e], yh_r.at[tc, place(at_z), e], other_yh).start()

    def from_yh(tc, at_z, e):
        arrived(feature(tc, 1, at_z, e), yh_s.at[tc, place(at_z), e], yh_r.at[tc, place(at_z), e])

    def send_z(tc, w, e):
        piece, j = feature(tc, w, z, e), chunk((yh + w) % 2, z, c) // 2
        for k in range(7):
            remote(piece, piece, z_s.at[tc, w, e, k], z_r.at[tc, j, e], along_z[k]).start()

    def tokens_own(tc, ref):
        @pl.when(holder)
        def _():
            feats[tc, home, yl] = ref[...]
            send_yh(tc, z, 0)
            if tc == 0:
                send_z(0, 0, 0)
            send_core(tc, 0, z, 0)

        @pl.when(jnp.logical_not(holder))
        def _():
            remote(ref, feats.at[tc, home, yl], yl_s.at[tc], yl_r.at[tc], other_yl).start()

    def tokens_second(tc):
        @pl.when(holder)
        def _():
            arrived(feature(tc, 0, z, 1), yl_s.at[tc], yl_r.at[tc])
            send_yh(tc, z, 1)
            if tc == 1:
                send_z(1, 0, 0)
            send_z(tc, 0, 1)
            send_core(tc, 0, z, 1)

    def cotangents_third():
        @pl.when(holder)
        def _():
            for e in range(2):
                from_yh(1, z, e)
                send_z(1, 1, e)
                send_core(1, 1, z, e)

    def from_z(tc, w):
        def step(i):
            e, at_z = i // 7, homes(i % 7 + 1)

            @pl.when(holds(at_z))
            def _():
                j = chunk((yh + w) % 2, at_z, c) // 2
                arrived(feature(tc, w, at_z, e), z_s.at[tc, w, e, 0], z_r.at[tc, j, e])
                if tc == 0:
                    send_yh(0, at_z, e)
                send_core(tc, w, at_z, e)

        loop(14, step)

    def tokens_from_yh():
        def step(i):
            e, at_z = i // 8, homes(i % 8)

            @pl.when(holds(at_z))
            def _():
                from_yh(0, at_z, e)
                send_core(0, 1, at_z, e)

        loop(16, step)

    def tokens_from_core(tc):
        def step(i):
            j, e = i // 2, i % 2
            arrived(feats.at[tc, j * 2 + 1 - c, (yl + e) % 2], c_s.at[tc, j, e], c_r.at[tc, j, e])

        loop(16, step)

    packed = (packed_0, packed_1, packed_2)
    masks, weights = (gate_m, up_m, down_m), (gate_w, up_w, down_w)
    lane = lax.broadcasted_iota(jnp.int32, (8, BLK), 0) * BLK + lax.broadcasted_iota(jnp.int32, (8, BLK), 1)

    def pack(m, table):
        for t in range(TILES):
            r, k = t // 4, t % 4
            tiles[t] = weights[m][r * BLK:(r + 1) * BLK, k * BLK:(k + 1) * BLK]
        count = jnp.int32(0)
        ids = [jnp.int32(0)] * SLOTS
        for t in range(TILES):
            kept = masks[m][t // 4, t % 4] > 0
            for s in range(min(t + 1, SLOTS)):
                ids[s] = jnp.where(jnp.logical_and(kept, count == s), t, ids[s])
            table = jnp.where(lane == m * BLK + t, jnp.where(kept, count, SLOTS), table)
            count = count + jnp.where(kept, 1, 0)
        for s in range(SLOTS):
            table = jnp.where(lane == m * BLK + TILES + s, ids[s], table)
            packed[m][x, s] = tiles[ids[s]]
        for at, to in ((0, x_right), (1, x_left)):
            for h in range(2):
                half = packed[m].at[x, pl.ds(h * 4, 4)]
                remote(half, half, ws_s.at[at, m, h], w_r.at[at, m, h], to).start()
        return table

    def forward_weights(m):
        for at, h, origin, to in ((0, 0, NX - 1, x_right), (1, 1, 1, x_left)):
            half = packed[m].at[(x + origin) % NX, pl.ds(h * 4, 4)]
            arrived(half, ws_s.at[at, m, h], w_r.at[at, m, h])
            remote(half, half, wf_s.at[m, h], w_r.at[2, m, h], to).start()

    def unpack(m):
        for at, origin in ((0, NX - 1), (1, 1), (2, 2)):
            for h in range(2):
                if at == 2 or at != h:
                    arrived(packed[m].at[(x + origin) % NX, pl.ds(h * 4, 4)], ws_s.at[0, m, h], w_r.at[at, m, h])

        def tile(i):
            xx, r = i // 4, i % 4
            for t in range(4):
                value = packed[m][xx, meta_sm[xx, m, r * 4 + t]]
                if m < 2:
                    row = pl.multiple_of(xx * 512 + r * BLK, BLK)
                    w_up[m, pl.ds(row, BLK), t * BLK:(t + 1) * BLK] = value
                else:
                    w_down[xx, pl.ds(pl.multiple_of(r * BLK, BLK), BLK), t * BLK:(t + 1) * BLK] = value

        loop(16, tile)

    tokens_own(0, tok)
    tokens_own(1, cot)
    table = pack(0, jnp.zeros((8, BLK), jnp.int32))
    tokens_second(0)
    table = pack(1, table)
    table = pack(2, table)
    meta[x] = table
    for at, to in ((0, x_right), (1, x_left), (2, x_far)):
        remote(meta.at[x], meta.at[x], meta_s.at[at], meta_r.at[at], to).start()
    tokens_second(1)
    cotangents_third()
    for xx in range(NX):
        for m in range(3):
            packed[m][xx, SLOTS] = jnp.zeros((BLK, BLK), BF16)
    from_z(0, 0)
    forward_weights(0)
    for at, origin in ((0, NX - 1), (1, 1), (2, 2)):
        arrived(meta.at[(x + origin) % NX], meta_s.at[at], meta_r.at[at])
    tables = pltpu.make_async_copy(meta, meta_sm, meta_l)
    tables.start()
    tokens_from_yh()
    tables.wait()
    unpack(0)
    forward_weights(1)

    def features(tc, h):
        return jnp.concatenate([feats[tc, q, h] for q in range(16)], axis=1)

    def exchange(m):
        def rows(h):
            if m < 2:
                total = jnp.dot(features(0, h), w_up[m], preferred_element_type=F32)
            else:
                total = jnp.zeros((256, 512), F32)
                for xx in range(NX):
                    left = jnp.concatenate([feats[1, xx * 4 + k, h] for k in range(4)], axis=1)
                    total += lax.dot_general(left, w_down[xx], (((1,), (1,)), ((), ())), preferred_element_type=F32)
            pre[m, h] = total
            psend[m, h] = total.astype(BF16)
            remote(psend.at[m, h], precv.at[m, h], p_s.at[m, h], p_r.at[m, h], other_yl).start()

        loop(2, rows)

    def exchanged(m):
        for h in range(2):
            arrived(precv.at[m, h], p_s.at[m, h], p_r.at[m, h])

    tokens_from_core(0)
    exchange(0)
    unpack(1)
    exchange(1)
    from_z(1, 0)
    forward_weights(2)
    from_z(1, 1)
    tokens_from_core(1)
    unpack(2)
    exchange(2)

    exchanged(0)
    exchanged(1)

    def activate(i):
        h, rows = i // 4, pl.ds(pl.multiple_of((i % 4) * 64, 64), 64)
        g = pre[0, h, rows, :] + precv[0, h, rows, :].astype(F32)
        u = pre[1, h, rows, :] + precv[1, h, rows, :].astype(F32)
        sigmoid = 1.0 / (1.0 + jnp.exp(-g))
        activated = g * sigmoid
        hid[h, rows, :] = (activated * u).astype(BF16)
        act[0, h, rows, :] = u * sigmoid * (1.0 + g * (1.0 - sigmoid))
        act[1, h, rows, :] = activated

    loop(8, activate)

    contract_rows = (((0,), (0,)), ((), ()))

    def grad_partial(m, rel):
        xx = (x + rel) % NX
        side = jnp.concatenate([feats[0 if m < 2 else 1, xx * 4 + k].reshape(512, BLK) for k in range(4)], axis=1)

        def col(k):
            if m < 2:
                right = deltas[m].reshape(512, 512)
                grad = lax.dot_general(side, right, contract_rows, preferred_element_type=F32)
            else:
                grad = lax.dot_general(hid[...].reshape(512, 512), side, contract_rows, preferred_element_type=F32)
            return grad

        grad = col(0).astype(BF16)
        for r in range(4):
            for t in range(4):
                tiles[r * 4 + t] = grad[r * BLK:(r + 1) * BLK, t * BLK:(t + 1) * BLK]
        for s in range(SLOTS):
            gpack[rel, m, s] = tiles[meta_sm[xx, m, TILES + s]]

    lows, highs = pl.ds(0, 4), pl.ds(4, 4)

    def grad_send(m, first=0, end=NX):
        def part(i, carry):
            rel = (i + 2) % NX
            grad_partial(m, rel)

            @pl.when(rel == 2)
            def _():
                remote(gpack.at[2, m, lows], gtransit.at[0, m], gt_s.at[0, m], gt_r.at[0, m], x_right).start()
                remote(gpack.at[2, m, highs], gtransit.at[1, m], gt_s.at[1, m], gt_r.at[1, m], x_left).start()

            @pl.when(rel == 1)
            def _():
                remote(gpack.at[1, m, highs], gfinal.at[0, m, highs], gf_s.at[0, m, 1], gf_r.at[0, m, 1], x_right).start()

            @pl.when(rel == 3)
            def _():
                remote(gpack.at[3, m, lows], gfinal.at[1, m, lows], gf_s.at[1, m, 0], gf_r.at[1, m, 0], x_left).start()

            return carry

        lax.fori_loop(first, end, part, 0)

    def grad_transit(m):
        for at, rel, h, to in ((0, 1, 0, x_right), (1, 3, 1, x_left)):
            part = pl.ds(h * 4, 4)
            arrived(gtransit.at[at, m], gt_s.at[at, m], gt_r.at[at, m])
            gpack[rel, m, part] = (gpack[rel, m, part].astype(F32) + gtransit[at, m].astype(F32)).astype(BF16)
            remote(gpack.at[rel, m, part], gfinal.at[at, m, part], gf_s.at[at, m, h], gf_r.at[at, m, h], to).start()

    def grad_finish(m, out):
        for at in range(2):
            for h in range(2):
                arrived(gfinal.at[at, m, pl.ds(h * 4, 4)], gf_s.at[at, m, h], gf_r.at[at, m, h])
        for s in range(SLOTS):
            total = gpack[0, m, s].astype(F32) + gfinal[0, m, s].astype(F32) + gfinal[1, m, s].astype(F32)
            gown[m, s] = (total * SCALE).astype(BF16)
        gown[m, SLOTS] = jnp.zeros((BLK, BLK), BF16)
        for t in range(TILES):
            r, k = t // 4, t % 4
            out[r * BLK:(r + 1) * BLK, k * BLK:(k + 1) * BLK] = gown[m, meta_sm[x, m, t]]

    def out_partial(o, w):
        at_yh = (yh + w) % 2

        def part(i):
            xx, h = at_yh * 2 + i // 2, i % 2
            if o == 0:
                term = jnp.dot(hid[h], w_down[xx], preferred_element_type=F32)
            else:
                rows = pl.ds(pl.multiple_of(xx * 512, 512), 512)
                along = (((1,), (1,)), ((), ()))
                term = lax.dot_general(deltas[0, h], w_up[0, rows, :], along, preferred_element_type=F32)
                term += lax.dot_general(deltas[1, h], w_up[1, rows, :], along, preferred_element_type=F32)
            term = term.astype(BF16)
            for k in range(4):
                outs[o, xx * 4 + k, h] = term[:, k * BLK:(k + 1) * BLK]

            @pl.when(h == 1)
            def _():
                for k in range(2):
                    j = xx * 2 + k
                    remote(outs.at[o, j * 2 + 1 - c], ocore.at[o, j], oc_s.at[o, j], oc_r.at[o, j], other_c).start()

        loop(4, part)

    def out_core(o, j):
        arrived(ocore.at[o, j], oc_s.at[o, j], oc_r.at[o, j])
        return outs[o, j * 2 + c].astype(F32) + ocore[o, j].astype(F32)

    def to_home(o, j, dst, send, recv):
        at_z = (j // 2) % 2 * 4 + yl * 2 + j % 2
        q = j * 2 + c

        @pl.when(at_z == z)
        def _():
            dst[...] = outs[o, q]

        for k, dz in enumerate((1, 7, 2, 6, 3, 5, 4)):

            @pl.when(at_z == (z + dz) % NZ)
            def _():
                remote(outs.at[o, q], dst, send, recv, along_z[k]).start()

    def layer_out_to_homes():
        def step(i):
            j = (i // 4 + yh + 1) % 2 * 4 + i % 4
            outs[0, j * 2 + c] = out_core(0, j).astype(BF16)
            to_home(0, j, oz_0.at[j // 4, z], oz_s.at[0, j], oz_r.at[0, j // 4, z])

        loop(8, step)

    def token_grad_to_yh():
        def step(i):
            j = (1 - yh) * 4 + i
            outs[1, j * 2 + c] = out_core(1, j).astype(BF16)
            remote(outs.at[1, j * 2 + c], oyh_1.at[i], oyh_s.at[1, i], oyh_r.at[1, i], other_yh).start()

        loop(4, step)

    def token_grad_to_homes():
        def step(i):
            j = yh * 4 + i
            total = out_core(1, j)
            arrived(oyh_1.at[i], oyh_s.at[1, i], oyh_r.at[1, i])
            outs[1, j * 2 + c] = (total + oyh_1[i].astype(F32)).astype(BF16)
            to_home(1, j, oz_1.at[z], oz_s.at[1, j], oz_r.at[1, 0, z])

        loop(4, step)

    def at_home(o, at_yh):
        def wait(i):
            at_z = homes(i + 1)
            dst = oz_0.at[at_yh, at_z] if o == 0 else oz_1.at[at_z]
            arrived(dst, oz_s.at[o, 0], oz_r.at[o, at_yh if o == 0 else 0, at_z])

        loop(7, wait)
        terms = oz_0.at[at_yh] if o == 0 else oz_1
        total = terms[0].astype(F32)
        for k in range(1, NZ):
            total += terms[k].astype(F32)
        return total

    def layer_out_yh():
        @pl.when(holder)
        def _():
            q = chunk(1 - yh, z, c)
            outs[0, q] = at_home(0, 1 - yh).astype(BF16)
            remote(outs.at[0, q], oyh_0, oyh_s.at[0, 0], oyh_r.at[0, 0], other_yh).start()

    def out_last(o, out):
        @pl.when(holder)
        def _():
            total = at_home(o, yh)
            if o == 0:
                arrived(oyh_0, oyh_s.at[0, 0], oyh_r.at[0, 0])
                total += oyh_0[...].astype(F32)
            outs[o, home] = total.astype(BF16)
            remote(outs.at[o, home, 1 - yl], oyl.at[o], oyl_s.at[o], oyl_r.at[o], other_yl).start()
            out[...] = outs[o, home, yl]

    def out_other(o, out):
        @pl.when(jnp.logical_not(holder))
        def _():
            arrived(oyl.at[o], oyl_s.at[o], oyl_r.at[o])
            out[...] = oyl[o]

    grad_send(2, 0, 1)
    out_partial(0, 1)
    out_partial(0, 0)
    grad_send(2, 1)
    layer_out_to_homes()
    grad_transit(2)
    exchanged(2)

    def delta(i):
        h, rows = i // 4, pl.ds(pl.multiple_of((i % 4) * 64, 64), 64)
        hg = pre[2, h, rows, :] + precv[2, h, rows, :].astype(F32)
        deltas[0, h, rows, :] = (hg * act[0, h, rows, :]).astype(BF16)
        deltas[1, h, rows, :] = (hg * act[1, h, rows, :]).astype(BF16)

    loop(8, delta)
    grad_send(0, 0, 1)
    out_partial(1, 1)
    out_partial(1, 0)
    grad_send(0, 1, 2)
    token_grad_to_yh()
    grad_send(0, 2)
    grad_send(1, 0, 1)
    grad_transit(0)
    token_grad_to_homes()
    grad_send(1, 1)
    grad_transit(1)
    layer_out_yh()
    out_last(0, layer_out)
    out_last(1, token_grad)
    grad_finish(2, down_g)
    grad_finish(0, gate_g)
    grad_finish(1, up_g)
    out_other(0, layer_out)
    out_other(1, token_grad)

    def left(src, send):
        remote(src, src, send, z_r.at[0, 0, 0], other_c).wait_send()

    piece, rows = feats.at[0, 0, 0], ocore.at[0, 0]

    def tokens_left(i):
        e, at_z = i // 8, homes(i % 8)

        @pl.when(holds(at_z))
        def _():
            left(piece, yh_s.at[0, place(at_z), e])

        j = i // 2
        for tc in range(2):
            left(piece, c_s.at[tc, j, i % 2])

        @pl.when(jnp.logical_not(jnp.logical_and(holder, (j // 2) % 2 * 4 + yl * 2 + j % 2 == z)))
        def _():
            @pl.when(i % 2 == 0)
            def _():
                left(rows, oz_s.at[0, j])

                @pl.when(j // 4 == yh)
                def _():
                    left(rows, oz_s.at[1, j])

        for o in range(2):

            @pl.when(i % 2 == o)
            def _():
                left(rows, oc_s.at[o, j])

    loop(16, tokens_left)

    def z_left(k):
        for e in range(2):
            for tc, w in ((0, 0), (1, 0), (1, 1)):
                left(piece, z_s.at[tc, w, e, k])

    for i in range(4):
        left(rows, oyh_s.at[1, i])

    @pl.when(holder)
    def _():
        loop(7, z_left)
        left(rows, oyh_s.at[0, 0])
        for o in range(2):
            left(piece, yh_s.at[1, place(z), o])
            left(piece, oyl_s.at[o])

    @pl.when(jnp.logical_not(holder))
    def _():
        for tc in range(2):
            left(piece, yl_s.at[tc])

    half = gtransit.at[0, 0]
    for at in range(3):
        left(meta.at[0], meta_s.at[at])
    for m in range(3):
        for h in range(2):
            for at in range(2):
                left(half, ws_s.at[at, m, h])
                left(half, gf_s.at[at, m, h])
            left(half, wf_s.at[m, h])
            left(half, gt_s.at[h, m])
            left(psend.at[0, 0], p_s.at[m, h])


def body(tokens, cotangent, gate_weight, up_weight, down_weight, gate_mask, up_mask, down_mask):
    vmem, smem = pl.BlockSpec(memory_space=pltpu.VMEM), pl.BlockSpec(memory_space=pltpu.SMEM)
    dma = pltpu.SemaphoreType.DMA
    shapes = (tokens, cotangent, gate_weight, up_weight, down_weight)
    return pl.pallas_call(
        kernel,
        out_shape=tuple(jax.ShapeDtypeStruct(a.shape, a.dtype) for a in shapes),
        in_specs=[vmem] * 5 + [smem] * 3,
        out_specs=(vmem,) * 5,
        scratch_shapes=[
            pltpu.VMEM((2, 16, 2, 256, BLK), BF16),
            *[pltpu.VMEM((NX, SLOTS + 1, BLK, BLK), BF16)] * 3,
            pltpu.VMEM((NX, 8, BLK), jnp.int32),
            pltpu.SMEM((NX, 8, BLK), jnp.int32),
            pltpu.VMEM((2, 2048, 512), BF16),
            pltpu.VMEM((NX, 512, 512), BF16),
            pltpu.VMEM((3, 2, 256, 512), F32),
            pltpu.VMEM((2, 2, 256, 512), F32),
            pltpu.VMEM((3, 2, 256, 512), BF16),
            pltpu.VMEM((3, 2, 256, 512), BF16),
            pltpu.VMEM((2, 256, 512), BF16),
            pltpu.VMEM((2, 2, 256, 512), BF16),
            pltpu.VMEM((TILES, BLK, BLK), BF16),
            pltpu.VMEM((NX, 3, SLOTS, BLK, BLK), BF16),
            pltpu.VMEM((2, 3, 4, BLK, BLK), BF16),
            pltpu.VMEM((2, 3, SLOTS, BLK, BLK), BF16),
            pltpu.VMEM((3, SLOTS + 1, BLK, BLK), BF16),
            pltpu.VMEM((2, 16, 2, 256, BLK), BF16),
            pltpu.VMEM((2, 8, 2, 256, BLK), BF16),
            pltpu.VMEM((2, NZ, 2, 256, BLK), BF16),
            pltpu.VMEM((NZ, 2, 256, BLK), BF16),
            pltpu.VMEM((2, 256, BLK), BF16),
            pltpu.VMEM((4, 2, 256, BLK), BF16),
            pltpu.VMEM((2, 256, BLK), BF16),
            dma((2,)), dma((2,)), dma((2, 4, 2)), dma((2, 4, 2)),
            dma((2, 2, 2, 7)), dma((2, 8, 2)),
            dma((2, 8, 2)), dma((2, 8, 2)),
            dma((2, 3, 2)), dma((3, 2)), dma((3, 3, 2)),
            dma((3,)), dma((3,)), dma(()),
            dma((3, 2)), dma((3, 2)),
            dma((2, 3)), dma((2, 3)), dma((2, 3, 2)), dma((2, 3, 2)),
            dma((2, 8)), dma((2, 8)),
            dma((2, 8)), dma((2, 2, NZ)),
            dma((2, 4)), dma((2, 4)), dma((2,)), dma((2,)),
        ],
        compiler_params=pltpu.CompilerParams(
            collective_id=0, has_side_effects=True, vmem_limit_bytes=58 * 2**20
        ),
        cost_estimate=pl.CostEstimate(flops=9_663_676_416, bytes_accessed=4 * 2**20, transcendentals=262144),
    )(tokens, cotangent, gate_weight, up_weight, down_weight, gate_mask, up_mask, down_mask)


def solution(mesh):
    up, down = P("dp", "mp"), P("mp", "dp")
    return jax.shard_map(
        body,
        mesh=mesh,
        in_specs=(up, up, up, up, down, up, up, down),
        out_specs=(up, up, up, up, down),
        check_vma=False,
    )
```

```python
import math

import jax
import jax.numpy as jnp
from jax import lax
from jax.experimental import pallas as pl
from jax.experimental.pallas import tpu as pltpu
from jax.sharding import PartitionSpec as P

BLK = 128
F32 = jnp.float32
BF16 = jnp.bfloat16
NX, NZ = 4, 8
SLOTS = 8
TILES = 16
SCALE = 1.0 / math.sqrt(2048)


def kernel(
    tok, cot, gate_w, up_w, down_w, gate_m, up_m, down_m,
    layer_out, token_grad, gown,
    feats, packed_0, packed_1, packed_2, meta, meta_sm, w_up, w_down, pre, act, psend, precv, hid, deltas,
    tiles, gpack, gtransit, gfinal, outs, ocore, oz_0, oz_1, oleaf, oyh_0, oyh_1, oyl,
    yl_s, yl_r, yh_s, yh_r, z_s, z_r, zf_s, zd_s, c_s, c_r,
    ws_s, wf_s, w_r, meta_s, meta_r, meta_l, p_s, p_r,
    gt_s, gt_r, gf_s, gf_r, oc_s, oc_r, oz_s, oz_r, ol_r, oyh_s, oyh_r, oyl_s, oyl_r,
):
    dp, mp = lax.axis_index("dp"), lax.axis_index("mp")
    x, yl = dp // 2, dp % 2
    yh, z, c = mp // 16, (mp % 16) // 2, mp % 2

    def dev(dx=0, dz=0, flip_yl=False, flip_yh=False, flip_c=False):
        yl_, yh_, c_ = (1 - yl if flip_yl else yl), (1 - yh if flip_yh else yh), (1 - c if flip_c else c)
        return (((x + dx) % NX) * 2 + yl_, yh_ * 16 + ((z + dz) % NZ) * 2 + c_)

    other_yl, other_yh, other_c = dev(flip_yl=True), dev(flip_yh=True), dev(flip_c=True)
    x_right, x_left, x_far = dev(dx=1), dev(dx=NX - 1), dev(dx=2)
    along_z = [dev(dz=k) for k in (1, 7, 2, 6, 3, 5, 4)]
    z_next = along_z[:2]

    def remote(src, dst, send, recv, to):
        return pltpu.make_async_remote_copy(
            src_ref=src, dst_ref=dst, send_sem=send, recv_sem=recv,
            device_id=to, device_id_type=pl.DeviceIdType.MESH,
        )

    def arrived(dst, send, recv):
        remote(dst, dst, send, recv, other_c).wait_recv()

    def loop(n, body):
        def step(i, carry):
            body(i)
            return carry

        lax.fori_loop(0, n, step, 0)

    barrier = pltpu.get_barrier_semaphore()
    partners = (other_yl, other_yh, other_c, x_right, x_left, x_far, *along_z)
    for to in partners:
        pl.semaphore_signal(barrier, inc=1, device_id=to, device_id_type=pl.DeviceIdType.MESH)
    pl.semaphore_wait(barrier, len(partners))

    holder = (z // 2) % 2 == yl

    def holds(at):
        return (at // 2) % 2 == yl

    def chunk(at_yh, at_z, at_c):
        return at_yh * 8 + (at_z // 4) * 4 + (at_z % 2) * 2 + at_c

    home = chunk(yh, z, c)

    def homes(i):
        return (z + jnp.where(i % 2 == 1, (i + 1) // 2, NZ - i // 2)) % NZ

    def feature(tc, w, at_z, e):
        return feats.at[tc, chunk((yh + w) % 2, at_z, c), (yl + e) % 2]

    def send_core(tc, w, at_z, e):
        piece, j = feature(tc, w, at_z, e), chunk((yh + w) % 2, at_z, c) // 2
        remote(piece, piece, c_s.at[tc, j, e], c_r.at[tc, j, e], other_c).start()

    def place(at_z):
        return (at_z // 4) * 2 + at_z % 2

    def send_yh(tc, at_z, e):
        piece = feature(tc, 0, at_z, e)
        remote(piece, piece, yh_s.at[tc, place(at_z), e], yh_r.at[tc, place(at_z), e], other_yh).start()

    def from_yh(tc, at_z, e):
        arrived(feature(tc, 1, at_z, e), yh_s.at[tc, place(at_z), e], yh_r.at[tc, place(at_z), e])

    def steps(e, k):
        return (k if e == 0 else NZ - k) % NZ

    def send_z(tc, w, e):
        piece, j = feature(tc, w, z, e), chunk((yh + w) % 2, z, c) // 2
        for d in range(2):
            remote(piece, piece, z_s.at[tc, w, e, d], z_r.at[tc, j, e], z_next[d]).start()

    def tokens_own(tc, ref):
        @pl.when(holder)
        def _():
            feats[tc, home, yl] = ref[...]
            send_yh(tc, z, 0)
            send_core(tc, 0, z, 0)
            if tc == 0:
                for k in range(7):
                    piece = feature(0, 0, z, 0)
                    remote(piece, piece, zd_s.at[k], z_r.at[0, home // 2, 0], along_z[6 - k]).start()

        @pl.when(jnp.logical_not(holder))
        def _():
            remote(ref, feats.at[tc, home, yl], yl_s.at[tc], yl_r.at[tc], other_yl).start()

    def tokens_second(tc):
        @pl.when(holder)
        def _():
            arrived(feature(tc, 0, z, 1), yl_s.at[tc], yl_r.at[tc])
            send_yh(tc, z, 1)
            if tc == 0:
                send_z(0, 0, 1)
            send_core(tc, 0, z, 1)

    def cotangents_third():
        @pl.when(holder)
        def _():
            for e in range(2):
                send_z(1, 0, e)
            for e in range(2):
                from_yh(1, z, e)
                send_z(1, 1, e)
                send_core(1, 1, z, e)

    def tokens_first():
        def step(i):
            at_z = homes(i + 1)

            @pl.when(holds(at_z))
            def _():
                arrived(feature(0, 0, at_z, 0), zd_s.at[0], z_r.at[0, chunk(yh, at_z, c) // 2, 0])
                send_yh(0, at_z, 0)
                send_core(0, 0, at_z, 0)

        loop(7, step)

    def z_hop(tc, hop):
        for w in range(1 + tc):
            for e in range(1 - tc, 2):
                for d in range(2):
                    last = 4 if e == d else 3
                    if hop > last:
                        continue
                    at_z = (z + (NZ - hop if d == 0 else hop)) % NZ

                    @pl.when(holds(at_z))
                    def _():
                        piece, j = feature(tc, w, at_z, e), chunk((yh + w) % 2, at_z, c) // 2
                        arrived(piece, zf_s.at[tc, j, e], z_r.at[tc, j, e])
                        if hop < last:
                            remote(piece, piece, zf_s.at[tc, j, e], z_r.at[tc, j, e], z_next[d]).start()
                        if tc == 0:
                            send_yh(0, at_z, e)
                        send_core(tc, w, at_z, e)

    def tokens_from_yh(e, first, end):
        def step(i, carry):
            at_z = homes(i)

            @pl.when(holds(at_z))
            def _():
                from_yh(0, at_z, e)
                send_core(0, 1, at_z, e)

            return carry

        lax.fori_loop(first, end, step, 0)

    def tokens_from_core(tc, e):
        def step(j):
            arrived(feats.at[tc, j * 2 + 1 - c, (yl + e) % 2], c_s.at[tc, j, e], c_r.at[tc, j, e])

        loop(8, step)

    packed = (packed_0, packed_1, packed_2)
    masks, weights = (gate_m, up_m, down_m), (gate_w, up_w, down_w)
    lane = lax.broadcasted_iota(jnp.int32, (8, BLK), 0) * BLK + lax.broadcasted_iota(jnp.int32, (8, BLK), 1)

    def pack(m, table):
        for t in range(TILES):
            r, k = t // 4, t % 4
            tiles[t] = weights[m][r * BLK:(r + 1) * BLK, k * BLK:(k + 1) * BLK]
        count = jnp.int32(0)
        ids = [jnp.int32(0)] * SLOTS
        for t in range(TILES):
            kept = masks[m][t // 4, t % 4] > 0
            for s in range(min(t + 1, SLOTS)):
                ids[s] = jnp.where(jnp.logical_and(kept, count == s), t, ids[s])
            table = jnp.where(lane == m * BLK + t, jnp.where(kept, count, SLOTS), table)
            count = count + jnp.where(kept, 1, 0)
        for s in range(SLOTS):
            table = jnp.where(lane == m * BLK + TILES + s, ids[s], table)
            packed[m][x, s] = tiles[ids[s]]
        return table

    def send_weights(m, part):
        for at, to in ((0, x_right), (1, x_left)):
            h = (at + part) % 2
            half = packed[m].at[x, pl.ds(h * 4, 4)]
            remote(half, half, ws_s.at[at, m, h], w_r.at[at, m, h], to).start()

    def forward_weights(m):
        for at, h, origin, to in ((0, 0, NX - 1, x_right), (1, 1, 1, x_left)):
            half = packed[m].at[(x + origin) % NX, pl.ds(h * 4, 4)]
            arrived(half, ws_s.at[at, m, h], w_r.at[at, m, h])
            remote(half, half, wf_s.at[m, h], w_r.at[2, m, h], to).start()

    def unpack(m):
        for at, origin in ((0, NX - 1), (1, 1), (2, 2)):
            for h in range(2):
                if at == 2 or at != h:
                    arrived(packed[m].at[(x + origin) % NX, pl.ds(h * 4, 4)], ws_s.at[0, m, h], w_r.at[at, m, h])

        def tile(i):
            xx, r = i // 4, i % 4
            for t in range(4):
                value = packed[m][xx, meta_sm[xx, m, r * 4 + t]]
                if m < 2:
                    row = pl.multiple_of(xx * 512 + r * BLK, BLK)
                    w_up[m, pl.ds(row, BLK), t * BLK:(t + 1) * BLK] = value
                else:
                    w_down[xx, pl.ds(pl.multiple_of(r * BLK, BLK), BLK), t * BLK:(t + 1) * BLK] = value

        loop(16, tile)

    tokens_own(0, tok)
    tokens_own(1, cot)
    table = pack(0, jnp.zeros((8, BLK), jnp.int32))
    send_weights(0, 0)
    send_weights(0, 1)
    tokens_second(0)
    table = pack(1, table)
    send_weights(1, 0)
    table = pack(2, table)
    meta[x] = table
    for at, to in ((0, x_right), (1, x_left), (2, x_far)):
        remote(meta.at[x], meta.at[x], meta_s.at[at], meta_r.at[at], to).start()
    for xx in range(NX):
        for m in range(3):
            packed[m][xx, SLOTS] = jnp.zeros((BLK, BLK), BF16)
    tokens_second(1)
    forward_weights(0)
    send_weights(1, 1)
    send_weights(2, 0)
    tokens_first()
    cotangents_third()
    z_hop(0, 1)
    forward_weights(1)
    send_weights(2, 1)
    tokens_from_yh(0, 0, 8)
    z_hop(0, 2)
    z_hop(1, 1)
    for at, origin in ((0, NX - 1), (1, 1), (2, 2)):
        arrived(meta.at[(x + origin) % NX], meta_s.at[at], meta_r.at[at])
    tables = pltpu.make_async_copy(meta, meta_sm, meta_l)
    tables.start()
    tables.wait()
    unpack(0)

    def features(tc, h):
        return jnp.concatenate([feats[tc, q, h] for q in range(16)], axis=1)

    def exchange(m, e):
        def rows(i):
            h = (yl + e) % 2
            if m < 2:
                total = jnp.dot(features(0, h), w_up[m], preferred_element_type=F32)
            else:
                total = jnp.zeros((256, 512), F32)
                for xx in range(NX):
                    left = jnp.concatenate([feats[1, xx * 4 + k, h] for k in range(4)], axis=1)
                    total += lax.dot_general(left, w_down[xx], (((1,), (1,)), ((), ())), preferred_element_type=F32)
            pre[m, h] = total
            psend[m, h] = total.astype(BF16)
            remote(psend.at[m, h], precv.at[m, h], p_s.at[m, h], p_r.at[m, h], other_yl).start()

        rows(0)

    def exchanged(m, e):
        h = (yl + e) % 2
        arrived(precv.at[m, h], p_s.at[m, h], p_r.at[m, h])

    tokens_from_core(0, 0)
    exchange(0, 0)
    z_hop(0, 3)
    z_hop(1, 2)
    forward_weights(2)
    z_hop(0, 4)
    unpack(1)
    exchange(1, 0)
    z_hop(1, 3)
    tokens_from_yh(1, 0, 8)
    z_hop(1, 4)
    tokens_from_core(0, 1)
    exchange(0, 1)
    exchange(1, 1)
    def activate(e):
        h = (yl + e) % 2

        def part(i):
            rows = pl.ds(pl.multiple_of(i * 64, 64), 64)
            g = pre[0, h, rows, :] + precv[0, h, rows, :].astype(F32)
            u = pre[1, h, rows, :] + precv[1, h, rows, :].astype(F32)
            sigmoid = 1.0 / (1.0 + jnp.exp(-g))
            activated = g * sigmoid
            hid[h, rows, :] = (activated * u).astype(BF16)
            act[0, h, rows, :] = u * sigmoid * (1.0 + g * (1.0 - sigmoid))
            act[1, h, rows, :] = activated

        exchanged(0, e)
        exchanged(1, e)
        loop(4, part)

    def delta(e):
        h = (yl + e) % 2

        def part(i):
            rows = pl.ds(pl.multiple_of(i * 64, 64), 64)
            hg = pre[2, h, rows, :] + precv[2, h, rows, :].astype(F32)
            deltas[0, h, rows, :] = (hg * act[0, h, rows, :]).astype(BF16)
            deltas[1, h, rows, :] = (hg * act[1, h, rows, :]).astype(BF16)

        exchanged(2, e)
        loop(4, part)

    contract_rows = (((0,), (0,)), ((), ()))

    def grad_partial(m, rel):
        xx = (x + rel) % NX
        side = jnp.concatenate([feats[0 if m < 2 else 1, xx * 4 + k].reshape(512, BLK) for k in range(4)], axis=1)

        def col(k):
            if m < 2:
                right = deltas[m].reshape(512, 512)
                grad = lax.dot_general(side, right, contract_rows, preferred_element_type=F32)
            else:
                grad = lax.dot_general(hid[...].reshape(512, 512), side, contract_rows, preferred_element_type=F32)
            return grad

        grad = col(0).astype(BF16)
        for r in range(4):
            for t in range(4):
                tiles[r * 4 + t] = grad[r * BLK:(r + 1) * BLK, t * BLK:(t + 1) * BLK]
        for s in range(SLOTS):
            gpack[rel, m, s] = tiles[meta_sm[xx, m, TILES + s]]

    lows, highs = pl.ds(0, 4), pl.ds(4, 4)

    def grad_send(m, first=0, end=NX):
        def part(i, carry):
            rel = (i + 2) % NX
            grad_partial(m, rel)

            @pl.when(rel == 2)
            def _():
                remote(gpack.at[2, m, lows], gtransit.at[0, m], gt_s.at[0, m], gt_r.at[0, m], x_right).start()
                remote(gpack.at[2, m, highs], gtransit.at[1, m], gt_s.at[1, m], gt_r.at[1, m], x_left).start()

            @pl.when(rel == 1)
            def _():
                remote(gpack.at[1, m, highs], gfinal.at[0, m, highs], gf_s.at[0, m, 1], gf_r.at[0, m, 1], x_right).start()

            @pl.when(rel == 3)
            def _():
                remote(gpack.at[3, m, lows], gfinal.at[1, m, lows], gf_s.at[1, m, 0], gf_r.at[1, m, 0], x_left).start()

            return carry

        lax.fori_loop(first, end, part, 0)

    def grad_transit(m):
        for at, rel, h, to in ((0, 1, 0, x_right), (1, 3, 1, x_left)):
            part = pl.ds(h * 4, 4)
            arrived(gtransit.at[at, m], gt_s.at[at, m], gt_r.at[at, m])
            gpack[rel, m, part] = (gpack[rel, m, part].astype(F32) + gtransit[at, m].astype(F32)).astype(BF16)
            remote(gpack.at[rel, m, part], gfinal.at[at, m, part], gf_s.at[at, m, h], gf_r.at[at, m, h], to).start()

    def grad_finish(m):
        for at in range(2):
            for h in range(2):
                arrived(gfinal.at[at, m, pl.ds(h * 4, 4)], gf_s.at[at, m, h], gf_r.at[at, m, h])
        for i in range(SLOTS):
            total = gpack[0, m, i].astype(F32) + gfinal[0, m, i].astype(F32) + gfinal[1, m, i].astype(F32)
            gown[m, i] = (total * SCALE).astype(BF16)
        gown[m, SLOTS] = jnp.zeros((BLK, BLK), BF16)

    def out_partial(o, w, e):
        at_yh, h = (yh + w) % 2, (yl + e) % 2

        def part(i):
            xx = at_yh * 2 + i
            if o == 0:
                term = jnp.dot(hid[h], w_down[xx], preferred_element_type=F32)
            else:
                rows = pl.ds(pl.multiple_of(xx * 512, 512), 512)
                along = (((1,), (1,)), ((), ()))
                term = lax.dot_general(deltas[0, h], w_up[0, rows, :], along, preferred_element_type=F32)
                term += lax.dot_general(deltas[1, h], w_up[1, rows, :], along, preferred_element_type=F32)
            term = term.astype(BF16)
            for k in range(4):
                outs[o, xx * 4 + k, h] = term[:, k * BLK:(k + 1) * BLK]
            for k in range(2):
                j = xx * 2 + k
                remote(outs.at[o, j * 2 + 1 - c, h], ocore.at[o, j, h], oc_s.at[o, j, h], oc_r.at[o, j, h], other_c).start()

        loop(2, part)

    def out_core(o, j, h):
        arrived(ocore.at[o, j, h], oc_s.at[o, j, h], oc_r.at[o, j, h])
        return outs[o, j * 2 + c, h].astype(F32) + ocore[o, j, h].astype(F32)

    def far(j, h):
        up = (z - ((j // 2) % 2 * 4 + yl * 2 + j % 2) + NZ) % NZ
        return jnp.where(h == 0, up, (NZ - up) % NZ)

    def on(h, k):
        return dev(dz=jnp.where(h == 0, k, NZ - k) % NZ)

    def to_home(o, j, h, k):
        slot = (1, 3, 6, 7).index(k)
        dst = oz_0.at[j // 4, slot, h] if o == 0 else oz_1.at[slot, h]
        recv = oz_r.at[o, j // 4 if o == 0 else 0, slot, h]
        remote(outs.at[o, j * 2 + c, h], dst, oz_s.at[o, j, h], recv, on(h, NZ - k)).start()

    def leaf(o, j, h):
        k = far(j, h)

        @pl.when(k == 7)
        def _():
            to_home(o, j, h, 7)

        @pl.when(jnp.logical_or(k == 5, jnp.logical_or(k == 4, k == 2)))
        def _():
            to = on(h, jnp.where(k == 5, 1, 7))
            remote(outs.at[o, j * 2 + c, h], oleaf.at[o, j, h], oz_s.at[o, j, h], ol_r.at[o, j, h], to).start()

    def relays(o, e):
        h = (yl + e) % 2

        def step(i):
            j = i if o == 0 else yh * 4 + i
            k, q = far(j, h), j * 2 + c

            @pl.when(jnp.logical_or(k == 6, jnp.logical_or(k == 3, k == 1)))
            def _():
                arrived(oleaf.at[o, j, h], oz_s.at[o, j, h], ol_r.at[o, j, h])
                outs[o, q, h] = (outs[o, q, h].astype(F32) + oleaf[o, j, h].astype(F32)).astype(BF16)
                for at in (1, 3, 6):

                    @pl.when(k == at)
                    def _():
                        to_home(o, j, h, at)

        loop(8 if o == 0 else 4, step)

    def layer_out_leaves(e):
        h = (yl + e) % 2

        def step(i):
            j = (i // 4 + yh + 1) % 2 * 4 + i % 4
            outs[0, j * 2 + c, h] = out_core(0, j, h).astype(BF16)
            leaf(0, j, h)

        loop(8, step)

    def token_grad_to_yh(e):
        h = (yl + e) % 2

        def step(i):
            j = (1 - yh) * 4 + i
            q = j * 2 + c
            outs[1, q, h] = out_core(1, j, h).astype(BF16)
            remote(outs.at[1, q, h], oyh_1.at[i, h], oyh_s.at[1, i, h], oyh_r.at[1, i, h], other_yh).start()

        loop(4, step)

    def token_grad_leaves(e):
        h = (yl + e) % 2

        def step(i):
            j = yh * 4 + i
            total = out_core(1, j, h)
            arrived(oyh_1.at[i, h], oyh_s.at[1, i, h], oyh_r.at[1, i, h])
            outs[1, j * 2 + c, h] = (total + oyh_1[i, h].astype(F32)).astype(BF16)
            leaf(1, j, h)

        loop(4, step)

    def at_home(o, at_yh):
        terms = oz_0.at[at_yh] if o == 0 else oz_1

        def wait(i):
            slot, h = i // 2, i % 2
            arrived(terms.at[slot, h], oz_s.at[o, 0, h], oz_r.at[o, at_yh if o == 0 else 0, slot, h])

        loop(8, wait)
        total = outs[o, chunk(at_yh, z, c)].astype(F32)
        for slot in range(4):
            total += terms[slot].astype(F32)
        return total

    def layer_out_yh():
        @pl.when(holder)
        def _():
            q = chunk(1 - yh, z, c)
            outs[0, q] = at_home(0, 1 - yh).astype(BF16)
            remote(outs.at[0, q], oyh_0, oyh_s.at[0, 0, 0], oyh_r.at[0, 0, 0], other_yh).start()

    def out_last(o, out):
        @pl.when(holder)
        def _():
            total = at_home(o, yh)
            if o == 0:
                arrived(oyh_0, oyh_s.at[0, 0, 0], oyh_r.at[0, 0, 0])
                total += oyh_0[...].astype(F32)
            outs[o, home] = total.astype(BF16)
            remote(outs.at[o, home, 1 - yl], oyl.at[o], oyl_s.at[o], oyl_r.at[o], other_yl).start()
            out[...] = outs[o, home, yl]

    def out_other(o, out):
        @pl.when(jnp.logical_not(holder))
        def _():
            arrived(oyl.at[o], oyl_s.at[o], oyl_r.at[o])
            out[...] = oyl[o]

    unpack(2)
    activate(0)
    out_partial(0, 1, 0)
    out_partial(0, 0, 0)
    tokens_from_core(1, 0)
    exchange(2, 0)
    tokens_from_core(1, 1)
    exchange(2, 1)
    layer_out_leaves(0)
    activate(1)
    out_partial(0, 1, 1)
    out_partial(0, 0, 1)
    relays(0, 0)
    grad_send(2, 0, 2)
    layer_out_leaves(1)
    grad_send(2, 2)
    grad_transit(2)
    delta(0)
    out_partial(1, 1, 0)
    out_partial(1, 0, 0)
    relays(0, 1)
    token_grad_to_yh(0)
    delta(1)
    out_partial(1, 1, 1)
    out_partial(1, 0, 1)
    grad_send(0, 0, 1)
    token_grad_to_yh(1)
    grad_send(0, 1, 2)
    grad_send(0, 3, 4)
    grad_send(1, 0, 1)
    token_grad_leaves(0)
    grad_send(1, 1, 2)
    grad_send(1, 3, 4)
    layer_out_yh()
    grad_transit(0)
    token_grad_leaves(1)
    relays(1, 0)
    grad_transit(1)
    grad_send(0, 2, 3)
    grad_send(1, 2, 3)
    relays(1, 1)
    out_last(0, layer_out)
    grad_finish(2)
    out_last(1, token_grad)
    grad_finish(0)
    grad_finish(1)
    out_other(0, layer_out)
    out_other(1, token_grad)

    def left(src, send):
        remote(src, src, send, z_r.at[0, 0, 0], other_c).wait_send()

    piece, rows = feats.at[0, 0, 0], ocore.at[0, 0]

    def tokens_left(i):
        e, at_z = i // 8, homes(i % 8)

        @pl.when(holds(at_z))
        def _():
            left(piece, yh_s.at[0, place(at_z), e])

        j = i // 2
        for tc in range(2):
            left(piece, c_s.at[tc, j, i % 2])

        @pl.when(jnp.logical_not(jnp.logical_and(holder, (j // 2) % 2 * 4 + yl * 2 + j % 2 == z)))
        def _():
            left(piece, oz_s.at[0, j, i % 2])

            @pl.when(j // 4 == yh)
            def _():
                left(piece, oz_s.at[1, j, i % 2])

        for o in range(2):
            left(piece, oc_s.at[o, j, i % 2])

    loop(16, tokens_left)

    for tc, w in ((0, 0), (1, 0), (1, 1)):
        for e in range(1 - tc, 2):
            for d in range(2):
                for hop in range(1, 4 if e == d else 3):
                    at_z = (z + (NZ - hop if d == 0 else hop)) % NZ

                    @pl.when(holds(at_z))
                    def _():
                        left(piece, zf_s.at[tc, chunk((yh + w) % 2, at_z, c) // 2, e])

    def z_left(k):
        for tc, w, e in ((0, 0, 1), (1, 0, 0), (1, 0, 1), (1, 1, 0), (1, 1, 1)):
            left(piece, z_s.at[tc, w, e, k])

    for i in range(4):
        for h in range(2):
            left(piece, oyh_s.at[1, i, h])

    @pl.when(holder)
    def _():
        loop(2, z_left)
        for k in range(7):
            left(piece, zd_s.at[k])
        left(rows, oyh_s.at[0, 0, 0])
        for o in range(2):
            left(piece, yh_s.at[1, place(z), o])
            left(piece, oyl_s.at[o])

    @pl.when(jnp.logical_not(holder))
    def _():
        for tc in range(2):
            left(piece, yl_s.at[tc])

    half = gtransit.at[0, 0]
    for at in range(3):
        left(meta.at[0], meta_s.at[at])
    for m in range(3):
        for h in range(2):
            for at in range(2):
                left(half, ws_s.at[at, m, h])
                left(half, gf_s.at[at, m, h])
            left(half, wf_s.at[m, h])
            left(half, gt_s.at[h, m])
            left(psend.at[0, 0], p_s.at[m, h])


def finish(out, grad, gown, gate_m, up_m, down_m, layer_out, token_grad, gate_g, up_g, down_g):
    layer_out[...] = out[...]
    token_grad[...] = grad[...]
    for m, (mask, dst) in enumerate(((gate_m, gate_g), (up_m, up_g), (down_m, down_g))):
        count = jnp.int32(0)
        for t in range(TILES):
            r, k = t // 4, t % 4
            kept = mask[r, k] > 0
            dst[r * BLK:(r + 1) * BLK, k * BLK:(k + 1) * BLK] = gown[m, jnp.where(kept, count, SLOTS)]
            count = count + jnp.where(kept, 1, 0)


def body(tokens, cotangent, gate_weight, up_weight, down_weight, gate_mask, up_mask, down_mask):
    vmem, smem = pl.BlockSpec(memory_space=pltpu.VMEM), pl.BlockSpec(memory_space=pltpu.SMEM)
    dma = pltpu.SemaphoreType.DMA
    shapes = (tokens, cotangent, gate_weight, up_weight, down_weight)
    shapes = tuple(jax.ShapeDtypeStruct(a.shape, a.dtype) for a in shapes)
    masks = (gate_mask, up_mask, down_mask)
    sums = pl.pallas_call(
        kernel,
        out_shape=(*shapes[:2], jax.ShapeDtypeStruct((3, SLOTS + 1, BLK, BLK), BF16)),
        in_specs=[vmem] * 5 + [smem] * 3,
        out_specs=(vmem,) * 3,
        scratch_shapes=[
            pltpu.VMEM((2, 16, 2, 256, BLK), BF16),
            *[pltpu.VMEM((NX, SLOTS + 1, BLK, BLK), BF16)] * 3,
            pltpu.VMEM((NX, 8, BLK), jnp.int32),
            pltpu.SMEM((NX, 8, BLK), jnp.int32),
            pltpu.VMEM((2, 2048, 512), BF16),
            pltpu.VMEM((NX, 512, 512), BF16),
            pltpu.VMEM((3, 2, 256, 512), F32),
            pltpu.VMEM((2, 2, 256, 512), F32),
            pltpu.VMEM((3, 2, 256, 512), BF16),
            pltpu.VMEM((3, 2, 256, 512), BF16),
            pltpu.VMEM((2, 256, 512), BF16),
            pltpu.VMEM((2, 2, 256, 512), BF16),
            pltpu.VMEM((TILES, BLK, BLK), BF16),
            pltpu.VMEM((NX, 3, SLOTS, BLK, BLK), BF16),
            pltpu.VMEM((2, 3, 4, BLK, BLK), BF16),
            pltpu.VMEM((2, 3, SLOTS, BLK, BLK), BF16),
            pltpu.VMEM((2, 16, 2, 256, BLK), BF16),
            pltpu.VMEM((2, 8, 2, 256, BLK), BF16),
            pltpu.VMEM((2, 4, 2, 256, BLK), BF16),
            pltpu.VMEM((4, 2, 256, BLK), BF16),
            pltpu.VMEM((2, 8, 2, 256, BLK), BF16),
            pltpu.VMEM((2, 256, BLK), BF16),
            pltpu.VMEM((4, 2, 256, BLK), BF16),
            pltpu.VMEM((2, 256, BLK), BF16),
            dma((2,)), dma((2,)), dma((2, 4, 2)), dma((2, 4, 2)),
            dma((2, 2, 2, 2)), dma((2, 8, 2)), dma((2, 8, 2)), dma((7,)),
            dma((2, 8, 2)), dma((2, 8, 2)),
            dma((2, 3, 2)), dma((3, 2)), dma((3, 3, 2)),
            dma((3,)), dma((3,)), dma(()),
            dma((3, 2)), dma((3, 2)),
            dma((2, 3)), dma((2, 3)), dma((2, 3, 2)), dma((2, 3, 2)),
            dma((2, 8, 2)), dma((2, 8, 2)),
            dma((2, 8, 2)), dma((2, 2, 4, 2)), dma((2, 8, 2)),
            dma((2, 4, 2)), dma((2, 4, 2)), dma((2,)), dma((2,)),
        ],
        compiler_params=pltpu.CompilerParams(
            collective_id=0, has_side_effects=True, vmem_limit_bytes=58 * 2**20
        ),
        cost_estimate=pl.CostEstimate(flops=9_663_676_416, bytes_accessed=4 * 2**20, transcendentals=262144),
    )(*(tokens, cotangent, gate_weight, up_weight, down_weight), *masks)
    return pl.pallas_call(
        finish, out_shape=shapes, in_specs=[vmem] * 3 + [smem] * 3, out_specs=(vmem,) * 5
    )(*sums, *masks)


def solution(mesh):
    up, down = P("dp", "mp"), P("mp", "dp")
    return jax.shard_map(
        body,
        mesh=mesh,
        in_specs=(up, up, up, up, down, up, up, down),
        out_specs=(up, up, up, up, down),
        check_vma=False,
    )
```

```python
import math

import jax
import jax.numpy as jnp
from jax import lax
from jax.experimental import pallas as pl
from jax.experimental.pallas import tpu as pltpu
from jax.sharding import PartitionSpec as P

BLK = 128
F32 = jnp.float32
BF16 = jnp.bfloat16
NX, NZ = 4, 8
SLOTS = 8
TILES = 16
SCALE = 1.0 / math.sqrt(2048)


def kernel(
    tok, cot, gate_w, up_w, down_w, gate_m, up_m, down_m,
    layer_out, token_grad, gown,
    feats, packed_0, packed_1, packed_2, meta, meta_sm, w_up, w_down, pre, act, psend, precv, hid, deltas,
    tiles, gpack, gtransit, gfinal, outs, ocore, oz_0, oz_1, oleaf, oyh_0, oyh_1, oyl,
    yl_s, yl_r, yh_s, yh_r, z_s, z_r, zf_s, zd_s, c_s, c_r,
    ws_s, wf_s, w_r, meta_s, meta_r, meta_l, p_s, p_r,
    gt_s, gt_r, gf_s, gf_r, oc_s, oc_r, oz_s, oz_r, ol_r, oyh_s, oyh_r, oyl_s, oyl_r,
):
    dp, mp = lax.axis_index("dp"), lax.axis_index("mp")
    x, yl = dp // 2, dp % 2
    yh, z, c = mp // 16, (mp % 16) // 2, mp % 2

    def dev(dx=0, dz=0, flip_yl=False, flip_yh=False, flip_c=False):
        yl_, yh_, c_ = (1 - yl if flip_yl else yl), (1 - yh if flip_yh else yh), (1 - c if flip_c else c)
        return (((x + dx) % NX) * 2 + yl_, yh_ * 16 + ((z + dz) % NZ) * 2 + c_)

    other_yl, other_yh, other_c = dev(flip_yl=True), dev(flip_yh=True), dev(flip_c=True)
    x_right, x_left, x_far = dev(dx=1), dev(dx=NX - 1), dev(dx=2)
    along_z = [dev(dz=k) for k in (1, 7, 2, 6, 3, 5, 4)]
    z_next = along_z[:2]

    def remote(src, dst, send, recv, to):
        return pltpu.make_async_remote_copy(
            src_ref=src, dst_ref=dst, send_sem=send, recv_sem=recv,
            device_id=to, device_id_type=pl.DeviceIdType.MESH,
        )

    def arrived(dst, send, recv):
        remote(dst, dst, send, recv, other_c).wait_recv()

    def loop(n, body):
        def step(i, carry):
            body(i)
            return carry

        lax.fori_loop(0, n, step, 0)

    barrier = pltpu.get_barrier_semaphore()
    partners = (other_yl, other_yh, other_c, x_right, x_left, x_far, *along_z)
    for to in partners:
        pl.semaphore_signal(barrier, inc=1, device_id=to, device_id_type=pl.DeviceIdType.MESH)
    pl.semaphore_wait(barrier, len(partners))

    holder = (z // 2) % 2 == yl

    def holds(at):
        return (at // 2) % 2 == yl

    def chunk(at_yh, at_z, at_c):
        return at_yh * 8 + (at_z // 4) * 4 + (at_z % 2) * 2 + at_c

    home = chunk(yh, z, c)

    def homes(i):
        return (z + jnp.where(i % 2 == 1, (i + 1) // 2, NZ - i // 2)) % NZ

    def feature(tc, w, at_z, e):
        return feats.at[tc, chunk((yh + w) % 2, at_z, c), (yl + e) % 2]

    def send_core(tc, w, at_z, e):
        piece, j = feature(tc, w, at_z, e), chunk((yh + w) % 2, at_z, c) // 2
        remote(piece, piece, c_s.at[tc, j, e], c_r.at[tc, j, e], other_c).start()

    def place(at_z):
        return (at_z // 4) * 2 + at_z % 2

    def send_yh(tc, at_z, e):
        piece = feature(tc, 0, at_z, e)
        remote(piece, piece, yh_s.at[tc, place(at_z), e], yh_r.at[tc, place(at_z), e], other_yh).start()

    def from_yh(tc, at_z, e):
        arrived(feature(tc, 1, at_z, e), yh_s.at[tc, place(at_z), e], yh_r.at[tc, place(at_z), e])

    def steps(e, k):
        return (k if e == 0 else NZ - k) % NZ

    def send_z(tc, w, e):
        piece, j = feature(tc, w, z, e), chunk((yh + w) % 2, z, c) // 2
        for d in range(2):
            remote(piece, piece, z_s.at[tc, w, e, d], z_r.at[tc, j, e], z_next[d]).start()

    def tokens_own(tc, ref):
        @pl.when(holder)
        def _():
            feats[tc, home, yl] = ref[...]
            send_yh(tc, z, 0)
            send_core(tc, 0, z, 0)
            if tc == 0:
                for k in range(7):
                    piece = feature(0, 0, z, 0)
                    remote(piece, piece, zd_s.at[k], z_r.at[0, home // 2, 0], along_z[6 - k]).start()

        @pl.when(jnp.logical_not(holder))
        def _():
            remote(ref, feats.at[tc, home, yl], yl_s.at[tc], yl_r.at[tc], other_yl).start()

    def tokens_second(tc):
        @pl.when(holder)
        def _():
            arrived(feature(tc, 0, z, 1), yl_s.at[tc], yl_r.at[tc])
            send_yh(tc, z, 1)
            if tc == 0:
                send_z(0, 0, 1)
            send_core(tc, 0, z, 1)

    def cotangents_third():
        @pl.when(holder)
        def _():
            for e in range(2):
                send_z(1, 0, e)
            for e in range(2):
                from_yh(1, z, e)
                send_z(1, 1, e)
                send_core(1, 1, z, e)

    def tokens_first():
        def step(i):
            at_z = homes(i + 1)

            @pl.when(holds(at_z))
            def _():
                arrived(feature(0, 0, at_z, 0), zd_s.at[0], z_r.at[0, chunk(yh, at_z, c) // 2, 0])
                send_yh(0, at_z, 0)
                send_core(0, 0, at_z, 0)

        loop(7, step)

    def z_hop(tc, hop):
        for w in range(1 + tc):
            for e in range(1 - tc, 2):
                for d in range(2):
                    last = 4 if e == d else 3
                    if hop > last:
                        continue
                    at_z = (z + (NZ - hop if d == 0 else hop)) % NZ

                    @pl.when(holds(at_z))
                    def _():
                        piece, j = feature(tc, w, at_z, e), chunk((yh + w) % 2, at_z, c) // 2
                        arrived(piece, zf_s.at[tc, j, e], z_r.at[tc, j, e])
                        if hop < last:
                            remote(piece, piece, zf_s.at[tc, j, e], z_r.at[tc, j, e], z_next[d]).start()
                        if tc == 0:
                            send_yh(0, at_z, e)
                        send_core(tc, w, at_z, e)

    def tokens_from_yh(e, first, end):
        def step(i, carry):
            at_z = homes(i)

            @pl.when(holds(at_z))
            def _():
                from_yh(0, at_z, e)
                send_core(0, 1, at_z, e)

            return carry

        lax.fori_loop(first, end, step, 0)

    def tokens_from_core(tc, e):
        def step(j):
            arrived(feats.at[tc, j * 2 + 1 - c, (yl + e) % 2], c_s.at[tc, j, e], c_r.at[tc, j, e])

        loop(8, step)

    packed = (packed_0, packed_1, packed_2)
    masks, weights = (gate_m, up_m, down_m), (gate_w, up_w, down_w)
    lane = lax.broadcasted_iota(jnp.int32, (8, BLK), 0) * BLK + lax.broadcasted_iota(jnp.int32, (8, BLK), 1)

    def pack(m, table):
        for t in range(TILES):
            r, k = t // 4, t % 4
            tiles[t] = weights[m][r * BLK:(r + 1) * BLK, k * BLK:(k + 1) * BLK]
        count = jnp.int32(0)
        ids = [jnp.int32(0)] * SLOTS
        for t in range(TILES):
            kept = masks[m][t // 4, t % 4] > 0
            for s in range(min(t + 1, SLOTS)):
                ids[s] = jnp.where(jnp.logical_and(kept, count == s), t, ids[s])
            table = jnp.where(lane == m * BLK + t, jnp.where(kept, count, SLOTS), table)
            count = count + jnp.where(kept, 1, 0)
        for s in range(SLOTS):
            table = jnp.where(lane == m * BLK + TILES + s, ids[s], table)
            packed[m][x, s] = tiles[ids[s]]
        return table

    def send_weights(m, part):
        for at, to in ((0, x_right), (1, x_left)):
            h = (at + part) % 2
            half = packed[m].at[x, pl.ds(h * 4, 4)]
            remote(half, half, ws_s.at[at, m, h], w_r.at[at, m, h], to).start()

    def forward_weights(m):
        for at, h, origin, to in ((0, 0, NX - 1, x_right), (1, 1, 1, x_left)):
            half = packed[m].at[(x + origin) % NX, pl.ds(h * 4, 4)]
            arrived(half, ws_s.at[at, m, h], w_r.at[at, m, h])
            remote(half, half, wf_s.at[m, h], w_r.at[2, m, h], to).start()

    def unpack(m):
        for at, origin in ((0, NX - 1), (1, 1), (2, 2)):
            for h in range(2):
                if at == 2 or at != h:
                    arrived(packed[m].at[(x + origin) % NX, pl.ds(h * 4, 4)], ws_s.at[0, m, h], w_r.at[at, m, h])

        def tile(i):
            xx, r = i // 4, i % 4
            for t in range(4):
                value = packed[m][xx, meta_sm[xx, m, r * 4 + t]]
                if m < 2:
                    row = pl.multiple_of(xx * 512 + r * BLK, BLK)
                    w_up[m, pl.ds(row, BLK), t * BLK:(t + 1) * BLK] = value
                else:
                    w_down[xx, pl.ds(pl.multiple_of(r * BLK, BLK), BLK), t * BLK:(t + 1) * BLK] = value

        loop(16, tile)

    tokens_own(0, tok)
    tokens_own(1, cot)
    table = pack(0, jnp.zeros((8, BLK), jnp.int32))
    send_weights(0, 0)
    send_weights(0, 1)
    tokens_second(0)
    table = pack(1, table)
    send_weights(1, 0)
    table = pack(2, table)
    meta[x] = table
    for at, to in ((0, x_right), (1, x_left), (2, x_far)):
        remote(meta.at[x], meta.at[x], meta_s.at[at], meta_r.at[at], to).start()
    for xx in range(NX):
        for m in range(3):
            packed[m][xx, SLOTS] = jnp.zeros((BLK, BLK), BF16)
    tokens_second(1)
    forward_weights(0)
    send_weights(1, 1)
    send_weights(2, 0)
    tokens_first()
    cotangents_third()
    z_hop(0, 1)
    forward_weights(1)
    send_weights(2, 1)
    tokens_from_yh(0, 0, 8)
    z_hop(0, 2)
    z_hop(1, 1)
    for at, origin in ((0, NX - 1), (1, 1), (2, 2)):
        arrived(meta.at[(x + origin) % NX], meta_s.at[at], meta_r.at[at])
    tables = pltpu.make_async_copy(meta, meta_sm, meta_l)
    tables.start()
    tables.wait()
    unpack(0)

    def features(tc, h):
        return jnp.concatenate([feats[tc, q, h] for q in range(16)], axis=1)

    def exchange(m, e):
        def rows(i):
            h = (yl + e) % 2
            if m < 2:
                total = jnp.dot(features(0, h), w_up[m], preferred_element_type=F32)
            else:
                total = jnp.zeros((256, 512), F32)
                for xx in range(NX):
                    left = jnp.concatenate([feats[1, xx * 4 + k, h] for k in range(4)], axis=1)
                    total += lax.dot_general(left, w_down[xx], (((1,), (1,)), ((), ())), preferred_element_type=F32)
            pre[m, h] = total
            psend[m, h] = total.astype(BF16)
            remote(psend.at[m, h], precv.at[m, h], p_s.at[m, h], p_r.at[m, h], other_yl).start()

        rows(0)

    def exchanged(m, e):
        h = (yl + e) % 2
        arrived(precv.at[m, h], p_s.at[m, h], p_r.at[m, h])

    tokens_from_core(0, 0)
    exchange(0, 0)
    z_hop(0, 3)
    z_hop(1, 2)
    forward_weights(2)
    z_hop(0, 4)
    unpack(1)
    exchange(1, 0)
    z_hop(1, 3)
    tokens_from_yh(1, 0, 8)
    z_hop(1, 4)
    tokens_from_core(0, 1)
    exchange(0, 1)
    exchange(1, 1)
    def activate(e):
        h = (yl + e) % 2

        def part(i):
            rows = pl.ds(pl.multiple_of(i * 64, 64), 64)
            g = pre[0, h, rows, :] + precv[0, h, rows, :].astype(F32)
            u = pre[1, h, rows, :] + precv[1, h, rows, :].astype(F32)
            sigmoid = 1.0 / (1.0 + jnp.exp(-g))
            activated = g * sigmoid
            hid[h, rows, :] = (activated * u).astype(BF16)
            act[0, h, rows, :] = u * sigmoid * (1.0 + g * (1.0 - sigmoid))
            act[1, h, rows, :] = activated

        exchanged(0, e)
        exchanged(1, e)
        loop(4, part)

    def delta(e):
        h = (yl + e) % 2

        def part(i):
            rows = pl.ds(pl.multiple_of(i * 64, 64), 64)
            hg = pre[2, h, rows, :] + precv[2, h, rows, :].astype(F32)
            deltas[0, h, rows, :] = (hg * act[0, h, rows, :]).astype(BF16)
            deltas[1, h, rows, :] = (hg * act[1, h, rows, :]).astype(BF16)

        exchanged(2, e)
        loop(4, part)

    contract_rows = (((0,), (0,)), ((), ()))

    def grad_partial(m, rel):
        xx = (x + rel) % NX
        side = jnp.concatenate([feats[0 if m < 2 else 1, xx * 4 + k].reshape(512, BLK) for k in range(4)], axis=1)

        def col(k):
            if m < 2:
                right = deltas[m].reshape(512, 512)
                grad = lax.dot_general(side, right, contract_rows, preferred_element_type=F32)
            else:
                grad = lax.dot_general(hid[...].reshape(512, 512), side, contract_rows, preferred_element_type=F32)
            return grad

        grad = col(0).astype(BF16)
        for r in range(4):
            for t in range(4):
                tiles[r * 4 + t] = grad[r * BLK:(r + 1) * BLK, t * BLK:(t + 1) * BLK]
        for s in range(SLOTS):
            gpack[rel, m, s] = tiles[meta_sm[xx, m, TILES + s]]

    lows, highs = pl.ds(0, 4), pl.ds(4, 4)

    def grad_send(m, first=0, end=NX):
        def part(i, carry):
            rel = (i + 2) % NX
            grad_partial(m, rel)

            @pl.when(rel == 2)
            def _():
                remote(gpack.at[2, m, lows], gtransit.at[0, m], gt_s.at[0, m], gt_r.at[0, m], x_right).start()
                remote(gpack.at[2, m, highs], gtransit.at[1, m], gt_s.at[1, m], gt_r.at[1, m], x_left).start()

            @pl.when(rel == 1)
            def _():
                remote(gpack.at[1, m, highs], gfinal.at[0, m, highs], gf_s.at[0, m, 1], gf_r.at[0, m, 1], x_right).start()

            @pl.when(rel == 3)
            def _():
                remote(gpack.at[3, m, lows], gfinal.at[1, m, lows], gf_s.at[1, m, 0], gf_r.at[1, m, 0], x_left).start()

            return carry

        lax.fori_loop(first, end, part, 0)

    def grad_transit(m):
        for at, rel, h, to in ((0, 1, 0, x_right), (1, 3, 1, x_left)):
            part = pl.ds(h * 4, 4)
            arrived(gtransit.at[at, m], gt_s.at[at, m], gt_r.at[at, m])
            gpack[rel, m, part] = (gpack[rel, m, part].astype(F32) + gtransit[at, m].astype(F32)).astype(BF16)
            remote(gpack.at[rel, m, part], gfinal.at[at, m, part], gf_s.at[at, m, h], gf_r.at[at, m, h], to).start()

    def grad_finish(m):
        for at in range(2):
            for h in range(2):
                arrived(gfinal.at[at, m, pl.ds(h * 4, 4)], gf_s.at[at, m, h], gf_r.at[at, m, h])
        for i in range(SLOTS):
            total = gpack[0, m, i].astype(F32) + gfinal[0, m, i].astype(F32) + gfinal[1, m, i].astype(F32)
            gown[m, i] = (total * SCALE).astype(BF16)
        gown[m, SLOTS] = jnp.zeros((BLK, BLK), BF16)

    def out_partial(o, w, e):
        at_yh, h = (yh + w) % 2, (yl + e) % 2

        def part(i):
            xx = at_yh * 2 + i
            if o == 0:
                term = jnp.dot(hid[h], w_down[xx], preferred_element_type=F32)
            else:
                rows = pl.ds(pl.multiple_of(xx * 512, 512), 512)
                along = (((1,), (1,)), ((), ()))
                term = lax.dot_general(deltas[0, h], w_up[0, rows, :], along, preferred_element_type=F32)
                term += lax.dot_general(deltas[1, h], w_up[1, rows, :], along, preferred_element_type=F32)
            term = term.astype(BF16)
            for k in range(4):
                outs[o, xx * 4 + k, h] = term[:, k * BLK:(k + 1) * BLK]
            for k in range(2):
                j = xx * 2 + k
                remote(outs.at[o, j * 2 + 1 - c, h], ocore.at[o, j, h], oc_s.at[o, j, h], oc_r.at[o, j, h], other_c).start()

        loop(2, part)

    def out_core(o, j, h):
        arrived(ocore.at[o, j, h], oc_s.at[o, j, h], oc_r.at[o, j, h])
        return outs[o, j * 2 + c, h].astype(F32) + ocore[o, j, h].astype(F32)

    def far(j, h):
        up = (z - ((j // 2) % 2 * 4 + yl * 2 + j % 2) + NZ) % NZ
        return jnp.where(h == 0, up, (NZ - up) % NZ)

    def on(h, k):
        return dev(dz=jnp.where(h == 0, k, NZ - k) % NZ)

    def to_home(o, j, h, k):
        slot = (1, 3, 6, 7).index(k)
        dst = oz_0.at[j // 4, slot, h] if o == 0 else oz_1.at[slot, h]
        recv = oz_r.at[o, j // 4 if o == 0 else 0, slot, h]
        remote(outs.at[o, j * 2 + c, h], dst, oz_s.at[o, j, h], recv, on(h, NZ - k)).start()

    def leaf(o, j, h):
        k = far(j, h)

        @pl.when(k == 7)
        def _():
            to_home(o, j, h, 7)

        @pl.when(jnp.logical_or(k == 5, jnp.logical_or(k == 4, k == 2)))
        def _():
            to = on(h, jnp.where(k == 5, 1, 7))
            remote(outs.at[o, j * 2 + c, h], oleaf.at[o, j, h], oz_s.at[o, j, h], ol_r.at[o, j, h], to).start()

    def relays(o, e):
        h = (yl + e) % 2

        def step(i):
            j = i if o == 0 else yh * 4 + i
            k, q = far(j, h), j * 2 + c

            @pl.when(jnp.logical_or(k == 6, jnp.logical_or(k == 3, k == 1)))
            def _():
                arrived(oleaf.at[o, j, h], oz_s.at[o, j, h], ol_r.at[o, j, h])
                outs[o, q, h] = (outs[o, q, h].astype(F32) + oleaf[o, j, h].astype(F32)).astype(BF16)
                for at in (1, 3, 6):

                    @pl.when(k == at)
                    def _():
                        to_home(o, j, h, at)

        loop(8 if o == 0 else 4, step)

    def layer_out_leaves(e):
        h = (yl + e) % 2

        def step(i):
            j = (i // 4 + yh + 1) % 2 * 4 + i % 4
            outs[0, j * 2 + c, h] = out_core(0, j, h).astype(BF16)
            leaf(0, j, h)

        loop(8, step)

    def token_grad_to_yh(e):
        h = (yl + e) % 2

        def step(i):
            j = (1 - yh) * 4 + i
            q = j * 2 + c
            outs[1, q, h] = out_core(1, j, h).astype(BF16)
            remote(outs.at[1, q, h], oyh_1.at[i, h], oyh_s.at[1, i, h], oyh_r.at[1, i, h], other_yh).start()

        loop(4, step)

    def token_grad_leaves(e):
        h = (yl + e) % 2

        def step(i):
            j = yh * 4 + i
            total = out_core(1, j, h)
            arrived(oyh_1.at[i, h], oyh_s.at[1, i, h], oyh_r.at[1, i, h])
            outs[1, j * 2 + c, h] = (total + oyh_1[i, h].astype(F32)).astype(BF16)
            leaf(1, j, h)

        loop(4, step)

    def at_home(o, at_yh):
        terms = oz_0.at[at_yh] if o == 0 else oz_1

        def wait(i):
            slot, h = i // 2, i % 2
            arrived(terms.at[slot, h], oz_s.at[o, 0, h], oz_r.at[o, at_yh if o == 0 else 0, slot, h])

        loop(8, wait)
        total = outs[o, chunk(at_yh, z, c)].astype(F32)
        for slot in range(4):
            total += terms[slot].astype(F32)
        return total

    def layer_out_yh():
        @pl.when(holder)
        def _():
            q = chunk(1 - yh, z, c)
            outs[0, q] = at_home(0, 1 - yh).astype(BF16)
            remote(outs.at[0, q], oyh_0, oyh_s.at[0, 0, 0], oyh_r.at[0, 0, 0], other_yh).start()

    def out_last(o, out):
        @pl.when(holder)
        def _():
            total = at_home(o, yh)
            if o == 0:
                arrived(oyh_0, oyh_s.at[0, 0, 0], oyh_r.at[0, 0, 0])
                total += oyh_0[...].astype(F32)
            outs[o, home] = total.astype(BF16)
            remote(outs.at[o, home, 1 - yl], oyl.at[o], oyl_s.at[o], oyl_r.at[o], other_yl).start()
            out[...] = outs[o, home, yl]

    def out_other(o, out):
        @pl.when(jnp.logical_not(holder))
        def _():
            arrived(oyl.at[o], oyl_s.at[o], oyl_r.at[o])
            out[...] = oyl[o]

    unpack(2)
    activate(0)
    out_partial(0, 1, 0)
    out_partial(0, 0, 0)
    tokens_from_core(1, 0)
    exchange(2, 0)
    tokens_from_core(1, 1)
    exchange(2, 1)
    layer_out_leaves(0)
    activate(1)
    out_partial(0, 1, 1)
    out_partial(0, 0, 1)
    grad_send(2, 0, 2)
    relays(0, 0)
    layer_out_leaves(1)
    grad_send(2, 2)
    grad_transit(2)
    delta(0)
    out_partial(1, 1, 0)
    out_partial(1, 0, 0)
    token_grad_to_yh(0)
    delta(1)
    out_partial(1, 1, 1)
    out_partial(1, 0, 1)
    relays(0, 1)
    grad_send(0, 0, 1)
    token_grad_to_yh(1)
    grad_send(0, 1, 2)
    grad_send(0, 3, 4)
    grad_send(1, 0, 1)
    token_grad_leaves(0)
    grad_send(1, 1, 2)
    grad_send(1, 3, 4)
    layer_out_yh()
    grad_transit(0)
    token_grad_leaves(1)
    relays(1, 0)
    grad_transit(1)
    grad_send(0, 2, 3)
    grad_send(1, 2, 3)
    relays(1, 1)
    out_last(0, layer_out)
    grad_finish(2)
    out_last(1, token_grad)
    grad_finish(0)
    grad_finish(1)
    out_other(0, layer_out)
    out_other(1, token_grad)

    def left(src, send):
        remote(src, src, send, z_r.at[0, 0, 0], other_c).wait_send()

    piece, rows = feats.at[0, 0, 0], ocore.at[0, 0]

    def tokens_left(i):
        e, at_z = i // 8, homes(i % 8)

        @pl.when(holds(at_z))
        def _():
            left(piece, yh_s.at[0, place(at_z), e])

        j = i // 2
        for tc in range(2):
            left(piece, c_s.at[tc, j, i % 2])

        @pl.when(jnp.logical_not(jnp.logical_and(holder, (j // 2) % 2 * 4 + yl * 2 + j % 2 == z)))
        def _():
            left(piece, oz_s.at[0, j, i % 2])

            @pl.when(j // 4 == yh)
            def _():
                left(piece, oz_s.at[1, j, i % 2])

        for o in range(2):
            left(piece, oc_s.at[o, j, i % 2])

    loop(16, tokens_left)

    for tc, w in ((0, 0), (1, 0), (1, 1)):
        for e in range(1 - tc, 2):
            for d in range(2):
                for hop in range(1, 4 if e == d else 3):
                    at_z = (z + (NZ - hop if d == 0 else hop)) % NZ

                    @pl.when(holds(at_z))
                    def _():
                        left(piece, zf_s.at[tc, chunk((yh + w) % 2, at_z, c) // 2, e])

    def z_left(k):
        for tc, w, e in ((0, 0, 1), (1, 0, 0), (1, 0, 1), (1, 1, 0), (1, 1, 1)):
            left(piece, z_s.at[tc, w, e, k])

    for i in range(4):
        for h in range(2):
            left(piece, oyh_s.at[1, i, h])

    @pl.when(holder)
    def _():
        loop(2, z_left)
        for k in range(7):
            left(piece, zd_s.at[k])
        left(rows, oyh_s.at[0, 0, 0])
        for o in range(2):
            left(piece, yh_s.at[1, place(z), o])
            left(piece, oyl_s.at[o])

    @pl.when(jnp.logical_not(holder))
    def _():
        for tc in range(2):
            left(piece, yl_s.at[tc])

    half = gtransit.at[0, 0]
    for at in range(3):
        left(meta.at[0], meta_s.at[at])
    for m in range(3):
        for h in range(2):
            for at in range(2):
                left(half, ws_s.at[at, m, h])
                left(half, gf_s.at[at, m, h])
            left(half, wf_s.at[m, h])
            left(half, gt_s.at[h, m])
            left(psend.at[0, 0], p_s.at[m, h])


def finish(out, grad, gown, gate_m, up_m, down_m, layer_out, token_grad, gate_g, up_g, down_g):
    layer_out[...] = out[...]
    token_grad[...] = grad[...]
    for m, (mask, dst) in enumerate(((gate_m, gate_g), (up_m, up_g), (down_m, down_g))):
        count = jnp.int32(0)
        for t in range(TILES):
            r, k = t // 4, t % 4
            kept = mask[r, k] > 0
            dst[r * BLK:(r + 1) * BLK, k * BLK:(k + 1) * BLK] = gown[m, jnp.where(kept, count, SLOTS)]
            count = count + jnp.where(kept, 1, 0)


def body(tokens, cotangent, gate_weight, up_weight, down_weight, gate_mask, up_mask, down_mask):
    vmem, smem = pl.BlockSpec(memory_space=pltpu.VMEM), pl.BlockSpec(memory_space=pltpu.SMEM)
    dma = pltpu.SemaphoreType.DMA
    shapes = (tokens, cotangent, gate_weight, up_weight, down_weight)
    shapes = tuple(jax.ShapeDtypeStruct(a.shape, a.dtype) for a in shapes)
    masks = (gate_mask, up_mask, down_mask)
    sums = pl.pallas_call(
        kernel,
        out_shape=(*shapes[:2], jax.ShapeDtypeStruct((3, SLOTS + 1, BLK, BLK), BF16)),
        in_specs=[vmem] * 5 + [smem] * 3,
        out_specs=(vmem,) * 3,
        scratch_shapes=[
            pltpu.VMEM((2, 16, 2, 256, BLK), BF16),
            *[pltpu.VMEM((NX, SLOTS + 1, BLK, BLK), BF16)] * 3,
            pltpu.VMEM((NX, 8, BLK), jnp.int32),
            pltpu.SMEM((NX, 8, BLK), jnp.int32),
            pltpu.VMEM((2, 2048, 512), BF16),
            pltpu.VMEM((NX, 512, 512), BF16),
            pltpu.VMEM((3, 2, 256, 512), F32),
            pltpu.VMEM((2, 2, 256, 512), F32),
            pltpu.VMEM((3, 2, 256, 512), BF16),
            pltpu.VMEM((3, 2, 256, 512), BF16),
            pltpu.VMEM((2, 256, 512), BF16),
            pltpu.VMEM((2, 2, 256, 512), BF16),
            pltpu.VMEM((TILES, BLK, BLK), BF16),
            pltpu.VMEM((NX, 3, SLOTS, BLK, BLK), BF16),
            pltpu.VMEM((2, 3, 4, BLK, BLK), BF16),
            pltpu.VMEM((2, 3, SLOTS, BLK, BLK), BF16),
            pltpu.VMEM((2, 16, 2, 256, BLK), BF16),
            pltpu.VMEM((2, 8, 2, 256, BLK), BF16),
            pltpu.VMEM((2, 4, 2, 256, BLK), BF16),
            pltpu.VMEM((4, 2, 256, BLK), BF16),
            pltpu.VMEM((2, 8, 2, 256, BLK), BF16),
            pltpu.VMEM((2, 256, BLK), BF16),
            pltpu.VMEM((4, 2, 256, BLK), BF16),
            pltpu.VMEM((2, 256, BLK), BF16),
            dma((2,)), dma((2,)), dma((2, 4, 2)), dma((2, 4, 2)),
            dma((2, 2, 2, 2)), dma((2, 8, 2)), dma((2, 8, 2)), dma((7,)),
            dma((2, 8, 2)), dma((2, 8, 2)),
            dma((2, 3, 2)), dma((3, 2)), dma((3, 3, 2)),
            dma((3,)), dma((3,)), dma(()),
            dma((3, 2)), dma((3, 2)),
            dma((2, 3)), dma((2, 3)), dma((2, 3, 2)), dma((2, 3, 2)),
            dma((2, 8, 2)), dma((2, 8, 2)),
            dma((2, 8, 2)), dma((2, 2, 4, 2)), dma((2, 8, 2)),
            dma((2, 4, 2)), dma((2, 4, 2)), dma((2,)), dma((2,)),
        ],
        compiler_params=pltpu.CompilerParams(
            collective_id=0, has_side_effects=True, vmem_limit_bytes=58 * 2**20
        ),
        cost_estimate=pl.CostEstimate(flops=9_663_676_416, bytes_accessed=4 * 2**20, transcendentals=262144),
    )(*(tokens, cotangent, gate_weight, up_weight, down_weight), *masks)
    return pl.pallas_call(
        finish, out_shape=shapes, in_specs=[vmem] * 3 + [smem] * 3, out_specs=(vmem,) * 5
    )(*sums, *masks)


def solution(mesh):
    up, down = P("dp", "mp"), P("mp", "dp")
    return jax.shard_map(
        body,
        mesh=mesh,
        in_specs=(up, up, up, up, down, up, up, down),
        out_specs=(up, up, up, up, down),
        check_vma=False,
    )
```

```python
import math

import jax
import jax.numpy as jnp
from jax import lax
from jax.experimental import pallas as pl
from jax.experimental.pallas import tpu as pltpu
from jax.sharding import PartitionSpec as P

BLK = 128
F32 = jnp.float32
BF16 = jnp.bfloat16
NX, NZ = 4, 8
SLOTS = 8
TILES = 16
SCALE = 1.0 / math.sqrt(2048)


def kernel(
    tok, cot, gate_w, up_w, down_w, gate_m, up_m, down_m,
    layer_out, token_grad, gown,
    feats, packed_0, packed_1, packed_2, meta, meta_sm, w_up, w_down, pre, act, psend, precv, hid, deltas,
    tiles, gpack, gtransit, gfinal, outs, ocore, oz_0, oz_1, oleaf, oyh_0, oyh_1, oyl,
    yl_s, yl_r, yh_s, yh_r, z_s, z_r, zf_s, zd_s, c_s, c_r,
    ws_s, wf_s, w_r, meta_s, meta_r, meta_l, p_s, p_r,
    gt_s, gt_r, gf_s, gf_r, oc_s, oc_r, oz_s, oz_r, ol_r, oyh_s, oyh_r, oyl_s, oyl_r,
):
    dp, mp = lax.axis_index("dp"), lax.axis_index("mp")
    x, yl = dp // 2, dp % 2
    yh, z, c = mp // 16, (mp % 16) // 2, mp % 2

    def dev(dx=0, dz=0, flip_yl=False, flip_yh=False, flip_c=False):
        yl_, yh_, c_ = (1 - yl if flip_yl else yl), (1 - yh if flip_yh else yh), (1 - c if flip_c else c)
        return (((x + dx) % NX) * 2 + yl_, yh_ * 16 + ((z + dz) % NZ) * 2 + c_)

    other_yl, other_yh, other_c = dev(flip_yl=True), dev(flip_yh=True), dev(flip_c=True)
    x_right, x_left, x_far = dev(dx=1), dev(dx=NX - 1), dev(dx=2)
    along_z = [dev(dz=k) for k in (1, 7, 2, 6, 3, 5, 4)]
    z_next = along_z[:2]

    def remote(src, dst, send, recv, to):
        return pltpu.make_async_remote_copy(
            src_ref=src, dst_ref=dst, send_sem=send, recv_sem=recv,
            device_id=to, device_id_type=pl.DeviceIdType.MESH,
        )

    def arrived(dst, send, recv):
        remote(dst, dst, send, recv, other_c).wait_recv()

    def loop(n, body):
        def step(i, carry):
            body(i)
            return carry

        lax.fori_loop(0, n, step, 0)

    barrier = pltpu.get_barrier_semaphore()
    partners = (other_yl, other_yh, other_c, x_right, x_left, x_far, *along_z)
    for to in partners:
        pl.semaphore_signal(barrier, inc=1, device_id=to, device_id_type=pl.DeviceIdType.MESH)
    pl.semaphore_wait(barrier, len(partners))

    holder = (z // 2) % 2 == yl

    def holds(at):
        return (at // 2) % 2 == yl

    def chunk(at_yh, at_z, at_c):
        return at_yh * 8 + (at_z // 4) * 4 + (at_z % 2) * 2 + at_c

    home = chunk(yh, z, c)

    def homes(i):
        return (z + jnp.where(i % 2 == 1, (i + 1) // 2, NZ - i // 2)) % NZ

    def feature(tc, w, at_z, e):
        return feats.at[tc, chunk((yh + w) % 2, at_z, c), (yl + e) % 2]

    def send_core(tc, w, at_z, e):
        piece, j = feature(tc, w, at_z, e), chunk((yh + w) % 2, at_z, c) // 2
        remote(piece, piece, c_s.at[tc, j, e], c_r.at[tc, j, e], other_c).start()

    def place(at_z):
        return (at_z // 4) * 2 + at_z % 2

    def send_yh(tc, at_z, e):
        piece = feature(tc, 0, at_z, e)
        remote(piece, piece, yh_s.at[tc, place(at_z), e], yh_r.at[tc, place(at_z), e], other_yh).start()

    def from_yh(tc, at_z, e):
        arrived(feature(tc, 1, at_z, e), yh_s.at[tc, place(at_z), e], yh_r.at[tc, place(at_z), e])

    def steps(e, k):
        return (k if e == 0 else NZ - k) % NZ

    def send_z(tc, w, e):
        piece, j = feature(tc, w, z, e), chunk((yh + w) % 2, z, c) // 2
        for d in range(2):
            remote(piece, piece, z_s.at[tc, w, e, d], z_r.at[tc, j, e], z_next[d]).start()

    def tokens_own(tc, ref):
        @pl.when(holder)
        def _():
            feats[tc, home, yl] = ref[...]
            send_yh(tc, z, 0)
            send_core(tc, 0, z, 0)
            if tc == 0:
                for k in range(7):
                    piece = feature(0, 0, z, 0)
                    remote(piece, piece, zd_s.at[k], z_r.at[0, home // 2, 0], along_z[6 - k]).start()

        @pl.when(jnp.logical_not(holder))
        def _():
            remote(ref, feats.at[tc, home, yl], yl_s.at[tc], yl_r.at[tc], other_yl).start()

    def tokens_second(tc):
        @pl.when(holder)
        def _():
            arrived(feature(tc, 0, z, 1), yl_s.at[tc], yl_r.at[tc])
            send_yh(tc, z, 1)
            if tc == 0:
                send_z(0, 0, 1)
            send_core(tc, 0, z, 1)

    def cotangents_third():
        @pl.when(holder)
        def _():
            for e in range(2):
                send_z(1, 0, e)
            for e in range(2):
                from_yh(1, z, e)
                send_z(1, 1, e)
                send_core(1, 1, z, e)

    def tokens_first():
        def step(i):
            at_z = homes(i + 1)

            @pl.when(holds(at_z))
            def _():
                arrived(feature(0, 0, at_z, 0), zd_s.at[0], z_r.at[0, chunk(yh, at_z, c) // 2, 0])
                send_yh(0, at_z, 0)
                send_core(0, 0, at_z, 0)

        loop(7, step)

    def z_hop(tc, hop):
        for w in range(1 + tc):
            for e in range(1 - tc, 2):
                for d in range(2):
                    last = 4 if e == d else 3
                    if hop > last:
                        continue
                    at_z = (z + (NZ - hop if d == 0 else hop)) % NZ

                    @pl.when(holds(at_z))
                    def _():
                        piece, j = feature(tc, w, at_z, e), chunk((yh + w) % 2, at_z, c) // 2
                        arrived(piece, zf_s.at[tc, j, e], z_r.at[tc, j, e])
                        if hop < last:
                            remote(piece, piece, zf_s.at[tc, j, e], z_r.at[tc, j, e], z_next[d]).start()
                        if tc == 0:
                            send_yh(0, at_z, e)
                        send_core(tc, w, at_z, e)

    def tokens_from_yh(e, first, end):
        def step(i, carry):
            at_z = homes(i)

            @pl.when(holds(at_z))
            def _():
                from_yh(0, at_z, e)
                send_core(0, 1, at_z, e)

            return carry

        lax.fori_loop(first, end, step, 0)

    def tokens_from_core(tc, e):
        def step(j):
            arrived(feats.at[tc, j * 2 + 1 - c, (yl + e) % 2], c_s.at[tc, j, e], c_r.at[tc, j, e])

        loop(8, step)

    packed = (packed_0, packed_1, packed_2)
    masks, weights = (gate_m, up_m, down_m), (gate_w, up_w, down_w)
    lane = lax.broadcasted_iota(jnp.int32, (8, BLK), 0) * BLK + lax.broadcasted_iota(jnp.int32, (8, BLK), 1)

    def pack(m, table):
        for t in range(TILES):
            r, k = t // 4, t % 4
            tiles[t] = weights[m][r * BLK:(r + 1) * BLK, k * BLK:(k + 1) * BLK]
        count = jnp.int32(0)
        ids = [jnp.int32(0)] * SLOTS
        for t in range(TILES):
            kept = masks[m][t // 4, t % 4] > 0
            for s in range(min(t + 1, SLOTS)):
                ids[s] = jnp.where(jnp.logical_and(kept, count == s), t, ids[s])
            table = jnp.where(lane == m * BLK + t, jnp.where(kept, count, SLOTS), table)
            count = count + jnp.where(kept, 1, 0)
        for s in range(SLOTS):
            table = jnp.where(lane == m * BLK + TILES + s, ids[s], table)
            packed[m][x, s] = tiles[ids[s]]
        return table

    def send_weights(m, part):
        for at, to in ((0, x_right), (1, x_left)):
            h = (at + part) % 2
            half = packed[m].at[x, pl.ds(h * 4, 4)]
            remote(half, half, ws_s.at[at, m, h], w_r.at[at, m, h], to).start()

    def forward_weights(m):
        for at, h, origin, to in ((0, 0, NX - 1, x_right), (1, 1, 1, x_left)):
            half = packed[m].at[(x + origin) % NX, pl.ds(h * 4, 4)]
            arrived(half, ws_s.at[at, m, h], w_r.at[at, m, h])
            remote(half, half, wf_s.at[m, h], w_r.at[2, m, h], to).start()

    def unpack(m):
        for at, origin in ((0, NX - 1), (1, 1), (2, 2)):
            for h in range(2):
                if at == 2 or at != h:
                    arrived(packed[m].at[(x + origin) % NX, pl.ds(h * 4, 4)], ws_s.at[0, m, h], w_r.at[at, m, h])

        def tile(i):
            xx, r = i // 4, i % 4
            for t in range(4):
                value = packed[m][xx, meta_sm[xx, m, r * 4 + t]]
                if m < 2:
                    row = pl.multiple_of(xx * 512 + r * BLK, BLK)
                    w_up[m, pl.ds(row, BLK), t * BLK:(t + 1) * BLK] = value
                else:
                    w_down[xx, pl.ds(pl.multiple_of(r * BLK, BLK), BLK), t * BLK:(t + 1) * BLK] = value

        loop(16, tile)

    tokens_own(0, tok)
    tokens_own(1, cot)
    table = pack(0, jnp.zeros((8, BLK), jnp.int32))
    send_weights(0, 0)
    send_weights(0, 1)
    tokens_second(0)
    table = pack(1, table)
    send_weights(1, 0)
    table = pack(2, table)
    meta[x] = table
    for at, to in ((0, x_right), (1, x_left), (2, x_far)):
        remote(meta.at[x], meta.at[x], meta_s.at[at], meta_r.at[at], to).start()
    for xx in range(NX):
        for m in range(3):
            packed[m][xx, SLOTS] = jnp.zeros((BLK, BLK), BF16)
    tokens_second(1)
    forward_weights(0)
    send_weights(1, 1)
    send_weights(2, 0)
    tokens_first()
    cotangents_third()
    z_hop(0, 1)
    forward_weights(1)
    send_weights(2, 1)
    tokens_from_yh(0, 0, 8)
    z_hop(0, 2)
    z_hop(1, 1)
    for at, origin in ((0, NX - 1), (1, 1), (2, 2)):
        arrived(meta.at[(x + origin) % NX], meta_s.at[at], meta_r.at[at])
    tables = pltpu.make_async_copy(meta, meta_sm, meta_l)
    tables.start()
    tables.wait()
    unpack(0)

    def features(tc, h):
        return jnp.concatenate([feats[tc, q, h] for q in range(16)], axis=1)

    def exchange(m, e):
        def rows(i):
            h = (yl + e) % 2
            if m < 2:
                total = jnp.dot(features(0, h), w_up[m], preferred_element_type=F32)
            else:
                total = jnp.zeros((256, 512), F32)
                for xx in range(NX):
                    left = jnp.concatenate([feats[1, xx * 4 + k, h] for k in range(4)], axis=1)
                    total += lax.dot_general(left, w_down[xx], (((1,), (1,)), ((), ())), preferred_element_type=F32)
            pre[m, h] = total
            psend[m, h] = total.astype(BF16)
            remote(psend.at[m, h], precv.at[m, h], p_s.at[m, h], p_r.at[m, h], other_yl).start()

        rows(0)

    def exchanged(m, e):
        h = (yl + e) % 2
        arrived(precv.at[m, h], p_s.at[m, h], p_r.at[m, h])

    tokens_from_core(0, 0)
    exchange(0, 0)
    z_hop(0, 3)
    z_hop(1, 2)
    forward_weights(2)
    z_hop(0, 4)
    unpack(1)
    exchange(1, 0)
    z_hop(1, 3)
    tokens_from_yh(1, 0, 8)
    z_hop(1, 4)
    tokens_from_core(0, 1)
    exchange(0, 1)
    exchange(1, 1)
    def activate(e):
        h = (yl + e) % 2

        def part(i):
            rows = pl.ds(pl.multiple_of(i * 64, 64), 64)
            g = pre[0, h, rows, :] + precv[0, h, rows, :].astype(F32)
            u = pre[1, h, rows, :] + precv[1, h, rows, :].astype(F32)
            sigmoid = 1.0 / (1.0 + jnp.exp(-g))
            activated = g * sigmoid
            hid[h, rows, :] = (activated * u).astype(BF16)
            act[0, h, rows, :] = u * sigmoid * (1.0 + g * (1.0 - sigmoid))
            act[1, h, rows, :] = activated

        exchanged(0, e)
        exchanged(1, e)
        loop(4, part)

    def delta(e):
        h = (yl + e) % 2

        def part(i):
            rows = pl.ds(pl.multiple_of(i * 64, 64), 64)
            hg = pre[2, h, rows, :] + precv[2, h, rows, :].astype(F32)
            deltas[0, h, rows, :] = (hg * act[0, h, rows, :]).astype(BF16)
            deltas[1, h, rows, :] = (hg * act[1, h, rows, :]).astype(BF16)

        exchanged(2, e)
        loop(4, part)

    contract_rows = (((0,), (0,)), ((), ()))

    def grad_partial(m, rel):
        xx = (x + rel) % NX
        side = jnp.concatenate([feats[0 if m < 2 else 1, xx * 4 + k].reshape(512, BLK) for k in range(4)], axis=1)

        def col(k):
            if m < 2:
                right = deltas[m].reshape(512, 512)
                grad = lax.dot_general(side, right, contract_rows, preferred_element_type=F32)
            else:
                grad = lax.dot_general(hid[...].reshape(512, 512), side, contract_rows, preferred_element_type=F32)
            return grad

        grad = col(0).astype(BF16)
        for r in range(4):
            for t in range(4):
                tiles[r * 4 + t] = grad[r * BLK:(r + 1) * BLK, t * BLK:(t + 1) * BLK]
        for s in range(SLOTS):
            gpack[rel, m, s] = tiles[meta_sm[xx, m, TILES + s]]

    lows, highs = pl.ds(0, 4), pl.ds(4, 4)

    def grad_send(m, first=0, end=NX):
        def part(i, carry):
            rel = (i + 2) % NX
            grad_partial(m, rel)

            @pl.when(rel == 2)
            def _():
                remote(gpack.at[2, m, lows], gtransit.at[0, m], gt_s.at[0, m], gt_r.at[0, m], x_right).start()
                remote(gpack.at[2, m, highs], gtransit.at[1, m], gt_s.at[1, m], gt_r.at[1, m], x_left).start()

            @pl.when(rel == 1)
            def _():
                remote(gpack.at[1, m, highs], gfinal.at[0, m, highs], gf_s.at[0, m, 1], gf_r.at[0, m, 1], x_right).start()

            @pl.when(rel == 3)
            def _():
                remote(gpack.at[3, m, lows], gfinal.at[1, m, lows], gf_s.at[1, m, 0], gf_r.at[1, m, 0], x_left).start()

            return carry

        lax.fori_loop(first, end, part, 0)

    def grad_transit(m):
        for at, rel, h, to in ((0, 1, 0, x_right), (1, 3, 1, x_left)):
            part = pl.ds(h * 4, 4)
            arrived(gtransit.at[at, m], gt_s.at[at, m], gt_r.at[at, m])
            gpack[rel, m, part] = (gpack[rel, m, part].astype(F32) + gtransit[at, m].astype(F32)).astype(BF16)
            remote(gpack.at[rel, m, part], gfinal.at[at, m, part], gf_s.at[at, m, h], gf_r.at[at, m, h], to).start()

    def grad_finish(m):
        for at in range(2):
            for h in range(2):
                arrived(gfinal.at[at, m, pl.ds(h * 4, 4)], gf_s.at[at, m, h], gf_r.at[at, m, h])
        for i in range(SLOTS):
            total = gpack[0, m, i].astype(F32) + gfinal[0, m, i].astype(F32) + gfinal[1, m, i].astype(F32)
            gown[m, i] = (total * SCALE).astype(BF16)
        gown[m, SLOTS] = jnp.zeros((BLK, BLK), BF16)

    def out_partial(o, w, e):
        at_yh, h = (yh + w) % 2, (yl + e) % 2

        def part(i):
            xx = at_yh * 2 + i
            if o == 0:
                term = jnp.dot(hid[h], w_down[xx], preferred_element_type=F32)
            else:
                rows = pl.ds(pl.multiple_of(xx * 512, 512), 512)
                along = (((1,), (1,)), ((), ()))
                term = lax.dot_general(deltas[0, h], w_up[0, rows, :], along, preferred_element_type=F32)
                term += lax.dot_general(deltas[1, h], w_up[1, rows, :], along, preferred_element_type=F32)
            term = term.astype(BF16)
            for k in range(4):
                outs[o, xx * 4 + k, h] = term[:, k * BLK:(k + 1) * BLK]
            for k in range(2):
                j = xx * 2 + k
                remote(outs.at[o, j * 2 + 1 - c, h], ocore.at[o, j, h], oc_s.at[o, j, h], oc_r.at[o, j, h], other_c).start()

        loop(2, part)

    def out_core(o, j, h):
        arrived(ocore.at[o, j, h], oc_s.at[o, j, h], oc_r.at[o, j, h])
        return outs[o, j * 2 + c, h].astype(F32) + ocore[o, j, h].astype(F32)

    def far(j, h):
        up = (z - ((j // 2) % 2 * 4 + yl * 2 + j % 2) + NZ) % NZ
        return jnp.where(h == 0, up, (NZ - up) % NZ)

    def on(h, k):
        return dev(dz=jnp.where(h == 0, k, NZ - k) % NZ)

    def to_home(o, j, h, k):
        slot = (1, 3, 6, 7).index(k)
        dst = oz_0.at[j // 4, slot, h] if o == 0 else oz_1.at[slot, h]
        recv = oz_r.at[o, j // 4 if o == 0 else 0, slot, h]
        remote(outs.at[o, j * 2 + c, h], dst, oz_s.at[o, j, h], recv, on(h, NZ - k)).start()

    def leaf(o, j, h):
        k = far(j, h)

        @pl.when(k == 7)
        def _():
            to_home(o, j, h, 7)

        @pl.when(jnp.logical_or(k == 5, jnp.logical_or(k == 4, k == 2)))
        def _():
            to = on(h, jnp.where(k == 5, 1, 7))
            remote(outs.at[o, j * 2 + c, h], oleaf.at[o, j, h], oz_s.at[o, j, h], ol_r.at[o, j, h], to).start()

    def relays(o, e):
        h = (yl + e) % 2

        def step(i):
            j = i if o == 0 else yh * 4 + i
            k, q = far(j, h), j * 2 + c

            @pl.when(jnp.logical_or(k == 6, jnp.logical_or(k == 3, k == 1)))
            def _():
                arrived(oleaf.at[o, j, h], oz_s.at[o, j, h], ol_r.at[o, j, h])
                outs[o, q, h] = (outs[o, q, h].astype(F32) + oleaf[o, j, h].astype(F32)).astype(BF16)
                for at in (1, 3, 6):

                    @pl.when(k == at)
                    def _():
                        to_home(o, j, h, at)

        loop(8 if o == 0 else 4, step)

    def layer_out_leaves(e):
        h = (yl + e) % 2

        def step(i):
            j = (i // 4 + yh + 1) % 2 * 4 + i % 4
            outs[0, j * 2 + c, h] = out_core(0, j, h).astype(BF16)
            leaf(0, j, h)

        loop(8, step)

    def token_grad_to_yh(e):
        h = (yl + e) % 2

        def step(i):
            j = (1 - yh) * 4 + i
            q = j * 2 + c
            outs[1, q, h] = out_core(1, j, h).astype(BF16)
            remote(outs.at[1, q, h], oyh_1.at[i, h], oyh_s.at[1, i, h], oyh_r.at[1, i, h], other_yh).start()

        loop(4, step)

    def token_grad_leaves(e):
        h = (yl + e) % 2

        def step(i):
            j = yh * 4 + i
            total = out_core(1, j, h)
            arrived(oyh_1.at[i, h], oyh_s.at[1, i, h], oyh_r.at[1, i, h])
            outs[1, j * 2 + c, h] = (total + oyh_1[i, h].astype(F32)).astype(BF16)
            leaf(1, j, h)

        loop(4, step)

    def at_home(o, at_yh):
        terms = oz_0.at[at_yh] if o == 0 else oz_1

        def wait(i):
            slot, h = i // 2, i % 2
            arrived(terms.at[slot, h], oz_s.at[o, 0, h], oz_r.at[o, at_yh if o == 0 else 0, slot, h])

        loop(8, wait)
        total = outs[o, chunk(at_yh, z, c)].astype(F32)
        for slot in range(4):
            total += terms[slot].astype(F32)
        return total

    def layer_out_yh():
        @pl.when(holder)
        def _():
            q = chunk(1 - yh, z, c)
            outs[0, q] = at_home(0, 1 - yh).astype(BF16)
            remote(outs.at[0, q], oyh_0, oyh_s.at[0, 0, 0], oyh_r.at[0, 0, 0], other_yh).start()

    def out_last(o, out):
        @pl.when(holder)
        def _():
            total = at_home(o, yh)
            if o == 0:
                arrived(oyh_0, oyh_s.at[0, 0, 0], oyh_r.at[0, 0, 0])
                total += oyh_0[...].astype(F32)
            outs[o, home] = total.astype(BF16)
            remote(outs.at[o, home, 1 - yl], oyl.at[o], oyl_s.at[o], oyl_r.at[o], other_yl).start()
            out[...] = outs[o, home, yl]

    def out_other(o, out):
        @pl.when(jnp.logical_not(holder))
        def _():
            arrived(oyl.at[o], oyl_s.at[o], oyl_r.at[o])
            out[...] = oyl[o]

    unpack(2)
    activate(0)
    out_partial(0, 1, 0)
    out_partial(0, 0, 0)
    tokens_from_core(1, 0)
    exchange(2, 0)
    tokens_from_core(1, 1)
    exchange(2, 1)
    layer_out_leaves(0)
    activate(1)
    out_partial(0, 1, 1)
    out_partial(0, 0, 1)
    grad_send(2, 0, 2)
    relays(0, 0)
    layer_out_leaves(1)
    grad_send(2, 2)
    grad_transit(2)
    delta(0)
    out_partial(1, 1, 0)
    out_partial(1, 0, 0)
    token_grad_to_yh(0)
    delta(1)
    out_partial(1, 1, 1)
    out_partial(1, 0, 1)
    relays(0, 1)
    grad_send(0, 0, 1)
    token_grad_to_yh(1)
    grad_send(0, 1, 2)
    grad_send(0, 3, 4)
    grad_send(1, 0, 1)
    grad_transit(0)
    token_grad_leaves(0)
    grad_send(1, 1, 2)
    grad_send(1, 3, 4)
    token_grad_leaves(1)
    layer_out_yh()
    grad_send(0, 2, 3)
    relays(1, 0)
    grad_transit(1)
    grad_send(1, 2, 3)
    relays(1, 1)
    out_last(0, layer_out)
    grad_finish(2)
    out_last(1, token_grad)
    grad_finish(0)
    grad_finish(1)
    out_other(0, layer_out)
    out_other(1, token_grad)

    def left(src, send):
        remote(src, src, send, z_r.at[0, 0, 0], other_c).wait_send()

    piece, rows = feats.at[0, 0, 0], ocore.at[0, 0]

    def tokens_left(i):
        e, at_z = i // 8, homes(i % 8)

        @pl.when(holds(at_z))
        def _():
            left(piece, yh_s.at[0, place(at_z), e])

        j = i // 2
        for tc in range(2):
            left(piece, c_s.at[tc, j, i % 2])

        @pl.when(jnp.logical_not(jnp.logical_and(holder, (j // 2) % 2 * 4 + yl * 2 + j % 2 == z)))
        def _():
            left(piece, oz_s.at[0, j, i % 2])

            @pl.when(j // 4 == yh)
            def _():
                left(piece, oz_s.at[1, j, i % 2])

        for o in range(2):
            left(piece, oc_s.at[o, j, i % 2])

    loop(16, tokens_left)

    for tc, w in ((0, 0), (1, 0), (1, 1)):
        for e in range(1 - tc, 2):
            for d in range(2):
                for hop in range(1, 4 if e == d else 3):
                    at_z = (z + (NZ - hop if d == 0 else hop)) % NZ

                    @pl.when(holds(at_z))
                    def _():
                        left(piece, zf_s.at[tc, chunk((yh + w) % 2, at_z, c) // 2, e])

    def z_left(k):
        for tc, w, e in ((0, 0, 1), (1, 0, 0), (1, 0, 1), (1, 1, 0), (1, 1, 1)):
            left(piece, z_s.at[tc, w, e, k])

    for i in range(4):
        for h in range(2):
            left(piece, oyh_s.at[1, i, h])

    @pl.when(holder)
    def _():
        loop(2, z_left)
        for k in range(7):
            left(piece, zd_s.at[k])
        left(rows, oyh_s.at[0, 0, 0])
        for o in range(2):
            left(piece, yh_s.at[1, place(z), o])
            left(piece, oyl_s.at[o])

    @pl.when(jnp.logical_not(holder))
    def _():
        for tc in range(2):
            left(piece, yl_s.at[tc])

    half = gtransit.at[0, 0]
    for at in range(3):
        left(meta.at[0], meta_s.at[at])
    for m in range(3):
        for h in range(2):
            for at in range(2):
                left(half, ws_s.at[at, m, h])
                left(half, gf_s.at[at, m, h])
            left(half, wf_s.at[m, h])
            left(half, gt_s.at[h, m])
            left(psend.at[0, 0], p_s.at[m, h])


def finish(out, grad, gown, gate_m, up_m, down_m, layer_out, token_grad, gate_g, up_g, down_g):
    layer_out[...] = out[...]
    token_grad[...] = grad[...]
    for m, (mask, dst) in enumerate(((gate_m, gate_g), (up_m, up_g), (down_m, down_g))):
        count = jnp.int32(0)
        for t in range(TILES):
            r, k = t // 4, t % 4
            kept = mask[r, k] > 0
            dst[r * BLK:(r + 1) * BLK, k * BLK:(k + 1) * BLK] = gown[m, jnp.where(kept, count, SLOTS)]
            count = count + jnp.where(kept, 1, 0)


def body(tokens, cotangent, gate_weight, up_weight, down_weight, gate_mask, up_mask, down_mask):
    vmem, smem = pl.BlockSpec(memory_space=pltpu.VMEM), pl.BlockSpec(memory_space=pltpu.SMEM)
    dma = pltpu.SemaphoreType.DMA
    shapes = (tokens, cotangent, gate_weight, up_weight, down_weight)
    shapes = tuple(jax.ShapeDtypeStruct(a.shape, a.dtype) for a in shapes)
    masks = (gate_mask, up_mask, down_mask)
    sums = pl.pallas_call(
        kernel,
        out_shape=(*shapes[:2], jax.ShapeDtypeStruct((3, SLOTS + 1, BLK, BLK), BF16)),
        in_specs=[vmem] * 5 + [smem] * 3,
        out_specs=(vmem,) * 3,
        scratch_shapes=[
            pltpu.VMEM((2, 16, 2, 256, BLK), BF16),
            *[pltpu.VMEM((NX, SLOTS + 1, BLK, BLK), BF16)] * 3,
            pltpu.VMEM((NX, 8, BLK), jnp.int32),
            pltpu.SMEM((NX, 8, BLK), jnp.int32),
            pltpu.VMEM((2, 2048, 512), BF16),
            pltpu.VMEM((NX, 512, 512), BF16),
            pltpu.VMEM((3, 2, 256, 512), F32),
            pltpu.VMEM((2, 2, 256, 512), F32),
            pltpu.VMEM((3, 2, 256, 512), BF16),
            pltpu.VMEM((3, 2, 256, 512), BF16),
            pltpu.VMEM((2, 256, 512), BF16),
            pltpu.VMEM((2, 2, 256, 512), BF16),
            pltpu.VMEM((TILES, BLK, BLK), BF16),
            pltpu.VMEM((NX, 3, SLOTS, BLK, BLK), BF16),
            pltpu.VMEM((2, 3, 4, BLK, BLK), BF16),
            pltpu.VMEM((2, 3, SLOTS, BLK, BLK), BF16),
            pltpu.VMEM((2, 16, 2, 256, BLK), BF16),
            pltpu.VMEM((2, 8, 2, 256, BLK), BF16),
            pltpu.VMEM((2, 4, 2, 256, BLK), BF16),
            pltpu.VMEM((4, 2, 256, BLK), BF16),
            pltpu.VMEM((2, 8, 2, 256, BLK), BF16),
            pltpu.VMEM((2, 256, BLK), BF16),
            pltpu.VMEM((4, 2, 256, BLK), BF16),
            pltpu.VMEM((2, 256, BLK), BF16),
            dma((2,)), dma((2,)), dma((2, 4, 2)), dma((2, 4, 2)),
            dma((2, 2, 2, 2)), dma((2, 8, 2)), dma((2, 8, 2)), dma((7,)),
            dma((2, 8, 2)), dma((2, 8, 2)),
            dma((2, 3, 2)), dma((3, 2)), dma((3, 3, 2)),
            dma((3,)), dma((3,)), dma(()),
            dma((3, 2)), dma((3, 2)),
            dma((2, 3)), dma((2, 3)), dma((2, 3, 2)), dma((2, 3, 2)),
            dma((2, 8, 2)), dma((2, 8, 2)),
            dma((2, 8, 2)), dma((2, 2, 4, 2)), dma((2, 8, 2)),
            dma((2, 4, 2)), dma((2, 4, 2)), dma((2,)), dma((2,)),
        ],
        compiler_params=pltpu.CompilerParams(
            collective_id=0, has_side_effects=True, vmem_limit_bytes=58 * 2**20
        ),
        cost_estimate=pl.CostEstimate(flops=9_663_676_416, bytes_accessed=4 * 2**20, transcendentals=262144),
    )(*(tokens, cotangent, gate_weight, up_weight, down_weight), *masks)
    return pl.pallas_call(
        finish, out_shape=shapes, in_specs=[vmem] * 3 + [smem] * 3, out_specs=(vmem,) * 5
    )(*sums, *masks)


def solution(mesh):
    up, down = P("dp", "mp"), P("mp", "dp")
    return jax.shard_map(
        body,
        mesh=mesh,
        in_specs=(up, up, up, up, down, up, up, down),
        out_specs=(up, up, up, up, down),
        check_vma=False,
    )
```
